32 devices in a mesh: dp: 16 (over z, y, core), vocab: 2 (over x).
Axes of the slice: x: 2, y: 2, z: 4, core: 2. Of those that a mesh axis runs over, the one named last changes fastest.
Arguments:
- hidden: bfloat16 [6144, 4096], P('dp'), may hold values from -6 to 6
- head_weight: bfloat16 [4096, 16000], P('dp', 'vocab'), may hold values from -0.09375 to 0.09375
- head_bias: float32 [16000], P('vocab'), may hold values from -3.5 to -1.5
- query_len: int32 [64], P('dp'), may hold values from 8 to 32
- passage_len: int32 [64], P('dp'), may hold values from 16 to 64
- neg_owner: int32 [64, 8], P('dp'), may hold values from 0 to 15, all different within a row; in each aligned block of 4 rows (0 to 3, 4 to 7, ...) at most 2 rows name the same one
- neg_index: int32 [64, 8], P('dp'), may hold values from 0 to 3
- teacher: float32 [64, 8], P('dp'), may hold values from -8 to 8
Outputs:
- margin_error: float32 [64, 8], P('dp')
- hidden_grad: float32 [6144, 4096], P(('dp', 'vocab'))
The draws below stay inside these ranges and needn't reach their ends.
Inputs may be any that keep to these rules, and one draw needn't show every extreme that they name: `neg_owner`: the 8 negatives of a query have different holders. Among the queries of one index of dp no holder appears more than 2 times, and in some of those blocks one holder appears exactly 2 times.
All inputs are finite; a program needn't handle non-finite values.
Results may differ from the reference program's by a relative error of at most 0.0028.
Values may be sent and summed in bfloat16 or wider, within the bound.
No kernel may reach another device: no remote copies, remote signals or barrier semaphores. Data moves between devices by JAX's collectives and lax.ppermute only.
A program may use at most 192 MiB of HBM per device.

```python
import math
import jax
import jax.numpy as jnp
import numpy as np
from jax import lax

D = 4096
VOCAB = 16000
Q_DEV = 4
LQ = 32
LP = 64
NEG = 8
CAP = 2
TOK_DEV = 384
QUERIES = 64
ROWS = 6144
N_DP = 16


def with_ends(result, key, least, largest):
    spot = [jax.random.randint(jax.random.fold_in(key, axis), (), 0, length) for axis, length in enumerate(result.shape)]
    main_axis = result.shape.index(max(result.shape))
    beside = spot[:main_axis] + [(spot[main_axis] + 1) % result.shape[main_axis]] + spot[main_axis + 1:]
    return result.at[tuple(spot)].set(least).at[tuple(beside)].set(largest)


def levels(own_key, dims, shards, least, top_value):
    loudness = 1.0
    for position, shards_of in shards:
        heights = jax.random.uniform(jax.random.fold_in(jax.random.fold_in(own_key, 6), position), (shards_of,), jnp.float32, least / len(shards), top_value / len(shards))
        loudness = loudness * jnp.repeat(jnp.exp(heights), dims[position] // shards_of).reshape((-1,) + (1,) * (len(dims) - 1 - position))
    return loudness


def deal_out(stream_key, own, number, rows, count, top, bound, slope):
    ranking = jax.random.permutation(stream_key, count)
    heavy_load, common = shares(count, rows * top, bound, slope, True), shares(count, rows * top, bound, slope, False)
    places = jnp.arange(count)

    def named(sizes, offset_by):
        used = int((sizes > 0).sum())
        fixed = max(1, used // 4)
        passed = fixed + (places - fixed + offset_by * (used - fixed)) % max(1, count - fixed)
        return jnp.zeros((count,), jnp.int32).at[ranking[jnp.where(places < fixed, places, passed)]].set(jnp.asarray(sizes, jnp.int32))

    sizes = jnp.where(number % 4 == 0, named(heavy_load, number // 4), named(common, number - number // 4 - 1))
    mixed = jax.random.permutation(jax.random.fold_in(own, 3), count)
    giver, taker = mixed[0:count // 2 * 2:2], mixed[1:count // 2 * 2:2]
    room = jnp.minimum(sizes[giver] - 1, bound - sizes[taker]) // 2
    room = jnp.where((giver == ranking[0]) | (taker == ranking[0]) | (sizes[taker] == 0), 0, jnp.maximum(room, 0))
    passed = jax.random.randint(jax.random.fold_in(own, 4), (count // 2,), 0, 1 << 20) % (room + 1)
    sizes = sizes.at[giver].add(-passed).at[taker].add(passed)
    items = jnp.searchsorted(jnp.cumsum(sizes), jnp.arange(rows * top), side="right").astype(jnp.int32)
    listing = items.reshape(top, rows).T
    listing = listing[jax.random.permutation(jax.random.fold_in(own, 1), rows)]
    offset_by = jax.random.randint(jax.random.fold_in(own, 2), (rows, 1), 0, top)
    return jnp.take_along_axis(listing, (jnp.arange(top)[None, :] + offset_by) % top, axis=1)


def shares(amount, total, bound, lean, full):
    portions = [(1 << 20) // math.isqrt(grade ** lean) + 1 for grade in range(1, amount + 1)]
    largest = bound if full else min(bound, max(-(-total // amount), total * portions[0] // sum(portions)))
    least = 1 if total - largest >= amount - 1 else 0
    given, spare = [largest] + [least] * (amount - 1), total - largest - least * (amount - 1)
    while spare > 0:
        movable = [i for i in range(1, amount) if given[i] < largest] or [i for i in range(1, amount) if given[i] < bound]
        mass, remaining = sum([portions[i] for i in movable]), spare
        for i in movable:
            more = min(bound - given[i], max(1, remaining * portions[i] // mass), spare)
            given[i] = given[i] + more
            spare = spare - more
    return np.array(given)


def scatter_about(key, shape, spread, reach, shards=(), dtype=jnp.bfloat16):
    loudness = levels(key, shape, shards, -0.22, 0.18) if shards else 1.0
    drawn = jax.random.normal(key, shape, jnp.float32) * spread * loudness
    return jnp.minimum(jnp.maximum(drawn, -reach), reach).astype(dtype)


def setup_inputs(seed: int = 0) -> dict:
    seeds = jax.random.split(jax.random.key(seed), 9)
    hidden = scatter_about(seeds[0], (ROWS, D), 1.0, 6.0, ((0, 16),))
    head_weight = scatter_about(seeds[1], (D, VOCAB), D ** -0.5, 0.09375, ((0, 16), (1, 2)))
    head_bias = jnp.clip(-3.5 + 2.0 * jax.random.uniform(seeds[2], (VOCAB,), jnp.float32) ** levels(seeds[2], (VOCAB,), ((0, 2),), -0.2, 0.2), -3.5, -1.5)
    query_len = with_ends(jax.random.randint(seeds[3], (QUERIES,), LQ // 4, LQ + 1), jax.random.fold_in(seeds[3], 1), LQ // 4, LQ).astype(jnp.int32)
    passage_len = with_ends(jax.random.randint(seeds[4], (QUERIES,), LP // 4, LP + 1), jax.random.fold_in(seeds[4], 1), LP // 4, LP).astype(jnp.int32)
    neg_owner_keys = jax.random.split(jax.random.fold_in(seeds[5], 1), QUERIES // Q_DEV)
    neg_owner_turns = jax.random.permutation(jax.random.fold_in(seeds[5], 3), QUERIES // Q_DEV)
    neg_owner = jax.vmap(lambda own, number: deal_out(jax.random.fold_in(seeds[5], 2), own, number, Q_DEV, N_DP, NEG, CAP, 2))(neg_owner_keys, neg_owner_turns).reshape((QUERIES, NEG))
    neg_index = with_ends(jax.random.randint(seeds[6], (QUERIES, NEG), 0, Q_DEV), jax.random.fold_in(seeds[6], 1), 0, Q_DEV - 1).astype(jnp.int32)
    teacher = scatter_about(seeds[7], (QUERIES, NEG), 2.0, 8.0, ((0, 16),), jnp.float32)
    return dict(hidden=hidden, head_weight=head_weight, head_bias=head_bias, query_len=query_len, passage_len=passage_len, neg_owner=neg_owner, neg_index=neg_index, teacher=teacher)


TAU = 0.05


def soft_pool(token_logits, token_mask):
    activation = jnp.log1p(jnp.maximum(token_logits, 0.0))
    weights = jnp.exp(activation / TAU) * token_mask[:, :, None]
    summed = jnp.sum(weights, axis=1)
    valid_count = jnp.sum(token_mask, axis=1)[:, None]
    return TAU * jnp.log(summed / valid_count), weights / summed[:, None, :]


def lengths_mask(lengths, span):
    return (jnp.arange(span)[None, :] < lengths[:, None]).astype(jnp.float32)


def block_logits(row_block, head_weight, head_bias):
    return jnp.dot(row_block, head_weight, preferred_element_type=jnp.float32) + head_bias[None, :]


def reference(hidden, head_weight, head_bias, query_len, passage_len, neg_owner, neg_index, teacher):
    blocks = hidden.reshape(N_DP, TOK_DEV, D)
    query_mask = lengths_mask(query_len, LQ).reshape(N_DP, Q_DEV, LQ)
    passage_mask = lengths_mask(passage_len, LP).reshape(N_DP, Q_DEV, LP)
    query_tokens = Q_DEV * LQ

    def forward(items):
        row_block, q_mask, p_mask = items
        logits = block_logits(row_block, head_weight, head_bias)
        query_rep, unused_q = soft_pool(logits[:query_tokens].reshape(Q_DEV, LQ, VOCAB), q_mask)
        passage_rep, unused_p = soft_pool(logits[query_tokens:].reshape(Q_DEV, LP, VOCAB), p_mask)
        return query_rep, passage_rep

    query_rep, passage_rep = lax.map(forward, (blocks, query_mask, passage_mask))
    query_rep = query_rep.reshape(QUERIES, VOCAB)
    passage_rep = passage_rep.reshape(QUERIES, VOCAB)
    passage_ids = (neg_owner * Q_DEV + neg_index).astype(jnp.int32)
    positive = jnp.sum(query_rep * passage_rep, axis=1)
    neg_rows = passage_rep[passage_ids]
    negative = jnp.sum(query_rep[:, None, :] * neg_rows, axis=2)
    margin_error = positive[:, None] - negative - teacher
    grad_pos = jnp.sum(margin_error, axis=1)
    grad_neg = -margin_error
    query_grad = grad_pos[:, None] * passage_rep + jnp.sum(grad_neg[:, :, None] * neg_rows, axis=1)
    neg_terms = (grad_neg[:, :, None] * query_rep[:, None, :]).reshape(-1, VOCAB)
    passage_grad = grad_pos[:, None] * query_rep + jax.ops.segment_sum(neg_terms, passage_ids.reshape(-1), num_segments=QUERIES)

    def backward(items):
        row_block, q_mask, p_mask, q_grad, p_grad = items
        logits = block_logits(row_block, head_weight, head_bias)
        unused_q, query_weights = soft_pool(logits[:query_tokens].reshape(Q_DEV, LQ, VOCAB), q_mask)
        unused_p, passage_weights = soft_pool(logits[query_tokens:].reshape(Q_DEV, LP, VOCAB), p_mask)
        relu_slope = (logits > 0).astype(jnp.float32) / (1.0 + jnp.maximum(logits, 0.0))
        d_query = (q_grad[:, None, :] * query_weights).reshape(-1, VOCAB)
        d_passage = (p_grad[:, None, :] * passage_weights).reshape(-1, VOCAB)
        logit_grad = (jnp.concatenate([d_query, d_passage], axis=0) * relu_slope).astype(jnp.bfloat16)
        return lax.dot_general(logit_grad, head_weight, (((1,), (1,)), ((), ())), preferred_element_type=jnp.float32)

    grads = lax.map(backward, (blocks, query_mask, passage_mask, query_grad.reshape(N_DP, Q_DEV, VOCAB), passage_grad.reshape(N_DP, Q_DEV, VOCAB)))
    return margin_error, grads.reshape(ROWS, D)
```

```python
import jax
import jax.numpy as jnp
from jax import lax
from jax.experimental import pallas as pl
from jax.experimental.pallas import tpu as pltpu
from jax.sharding import PartitionSpec as P

LQ = 32
LP = 64


TAU = 0.05
AXES = ("dp", "vocab")
F32 = jnp.float32
BF16 = jnp.bfloat16
X, CORE, Y, ZLO, ZHI = 1, 2, 4, 8, 16
ORDER = (0, 4, 8, 12, 2, 6, 10, 14, 1, 5, 9, 13, 3, 7, 11, 15)
CHUNKS = (256,) + (512,) * 7 + (160,)
NEAR = {0: (0,), 1: (1, 2), 3: (3, 4), 5: (5, 6), 7: (7, 8)}
HIDDEN = (2, 4)
TABLE = {0: ZLO, 1: ZHI, 6: Y, 8: CORE}
EARLY = {10: ZHI, 11: Y, 12: CORE}
EARLY_GROUPS = 4
GROUPS = ((0,), (1, 2), (3,), (4,), (5,), (6,), (7,), (8,))
PACKED = (3, 5, 6, 7, 8, 9, 10, 11)
MOVED = (4, 6, 7, 8, 9, 10, 10, 11)
COMPUTED = (6, 7, 8, 9, 10, 11, 11, 12)
HIGHEST = lax.Precision.HIGHEST
NO_COST = pl.CostEstimate(flops=0, bytes_accessed=0, transcendentals=0)


def soft_pool(token_logits, token_mask):
    activation = jnp.log1p(jnp.maximum(token_logits, 0.0))
    weights = jnp.exp(activation / TAU) * token_mask[:, :, None]
    summed = jnp.sum(weights, axis=1)
    valid_count = jnp.sum(token_mask, axis=1)[:, None]
    return (TAU * jnp.log(summed / valid_count), weights / summed[:, None, :])


def lengths_mask(lengths, span):
    return (jnp.arange(span)[None, :] < lengths[:, None]).astype(jnp.float32)


def any_mesh(
    hidden, head_weight, head_bias, query_len, passage_len, neg_owner, neg_index, teacher
):
    query_count = neg_owner.shape[0]
    neg_count = neg_owner.shape[1]
    owners = lax.axis_size("dp")
    head_full = lax.all_gather(head_weight, "dp", axis=0, tiled=True)
    vocab_width = head_full.shape[1]
    logits = jnp.dot(hidden, head_full, preferred_element_type=jnp.float32) + head_bias[None, :]
    query_tokens = query_count * LQ
    query_rep, query_weights = soft_pool(
        logits[:query_tokens].reshape(query_count, LQ, vocab_width), lengths_mask(query_len, LQ)
    )
    passage_rep, passage_weights = soft_pool(
        logits[query_tokens:].reshape(query_count, LP, vocab_width), lengths_mask(passage_len, LP)
    )
    gathered = lax.all_gather(passage_rep, "dp", axis=0, tiled=True)
    passage_ids = neg_owner * query_count + neg_index
    neg_rows = jnp.take(gathered, passage_ids.reshape(-1), axis=0).reshape(
        query_count, neg_count, vocab_width
    )
    pos_part = jnp.sum(query_rep * passage_rep, axis=1)
    neg_part = jnp.sum(query_rep[:, None, :] * neg_rows, axis=2)
    positive, negative = lax.psum((pos_part, neg_part), "vocab")
    margin_error = positive[:, None] - negative - teacher
    grad_pos = jnp.sum(margin_error, axis=1)
    grad_neg = -margin_error
    query_grad = grad_pos[:, None] * passage_rep + jnp.sum(grad_neg[:, :, None] * neg_rows, axis=1)
    neg_terms = (grad_neg[:, :, None] * query_rep[:, None, :]).reshape(-1, vocab_width)
    scattered = jax.ops.segment_sum(
        neg_terms, passage_ids.reshape(-1), num_segments=owners * query_count
    )
    returned_grad = lax.psum_scatter(scattered, "dp", scatter_dimension=0, tiled=True)
    passage_grad = grad_pos[:, None] * query_rep + returned_grad
    relu_slope = (logits > 0).astype(jnp.float32) / (1.0 + jnp.maximum(logits, 0.0))
    d_query = (query_grad[:, None, :] * query_weights).reshape(-1, vocab_width)
    d_passage = (passage_grad[:, None, :] * passage_weights).reshape(-1, vocab_width)
    logit_grad = (jnp.concatenate([d_query, d_passage], axis=0) * relu_slope).astype(jnp.bfloat16)
    hidden_grad = lax.psum_scatter(
        lax.dot_general(
            logit_grad, head_full, (((1,), (1,)), ((), ())), preferred_element_type=jnp.float32
        ),
        "vocab",
        scatter_dimension=0,
        tiled=True,
    )
    return (margin_error, hidden_grad)


def in_hbm(*arrays):
    return [pltpu.with_memory_space_constraint(a, pltpu.HBM) for a in arrays]


def in_vmem(array):
    return pltpu.with_memory_space_constraint(array, pltpu.VMEM)


def swap(array, bits):
    return lax.ppermute(array, AXES, [(i, i ^ bits) for i in range(32)])


def arrange(places, hidden, other):
    rows, width = hidden.shape
    block = width // 16
    step = 128
    n = rows // step

    def kernel(places, a, b, out):
        def put(source):
            for k in range(16):
                lanes = pl.ds(pl.multiple_of(places[k] * block, block), block)
                out[:, k * block : (k + 1) * block] = source[:, lanes]

        own = places[0] // 4 % 2
        here = pl.program_id(0) // n == own

        @pl.when(here)
        def _():
            put(a)

        @pl.when(jnp.logical_not(here))
        def _():
            put(b)

    def at(turn):
        def index(i, places):
            first = (places[0] // 4 + turn) % 2 * n
            return jnp.clip(i - first, 0, n - 1), 0

        return pl.BlockSpec((step, width), index)

    return pl.pallas_call(
        kernel,
        grid_spec=pltpu.PrefetchScalarGridSpec(
            num_scalar_prefetch=1,
            grid=(2 * n,),
            in_specs=[at(0), at(1)],
            out_specs=pl.BlockSpec((step, width), lambda i, places: (i, 0)),
        ),
        out_shape=pltpu.VMEM((2 * rows, width), hidden.dtype),
        compiler_params=pltpu.CompilerParams(vmem_limit_bytes=40 * 2**20),
        cost_estimate=NO_COST,
        name="arrange",
    )(places, hidden, other)


def pack(groups):
    n = len(groups)
    width = groups[0][0].shape[1]
    heights = [group[0].shape[0] for group in groups]
    step = 128 if all(h % 128 == 0 for h in heights) else heights[0]
    ends = [sum(heights[: i + 1]) // step for i in range(n)]
    firsts = [0] + ends[:-1]

    def kernel(*refs):
        out = refs[-1]
        for i in range(n):

            @pl.when((pl.program_id(0) >= firsts[i]) & (pl.program_id(0) < ends[i]))
            def _():
                for k in range(4):
                    out[:, k * width : (k + 1) * width] = refs[4 * i + k][...]

    specs = []
    for i in range(n):
        last = heights[i] // step - 1
        specs += [
            pl.BlockSpec((step, width), lambda r, i=i, last=last: (jnp.clip(r - firsts[i], 0, last), 0))
        ] * 4
    return pl.pallas_call(
        kernel,
        grid=(ends[-1],),
        in_specs=specs,
        out_specs=pl.BlockSpec((step, 4 * width), lambda r: (r, 0)),
        out_shape=pltpu.HBM((sum(heights), 4 * width), BF16),
        compiler_params=pltpu.CompilerParams(vmem_limit_bytes=40 * 2**20),
        cost_estimate=NO_COST,
        name="pack",
    )(*in_hbm(*[a for group in groups for a in group]))


def forward(lens, rows, near, across, bias, slopes, start):
    tokens, depth = rows.shape
    wide, deep = near.shape
    tile = 256
    tiles = -(-wide // tile)
    count = lens.shape[0] // 4
    spans = [LQ] * count + [LP] * count

    def kernel(lens, rows, near, across, bias, *refs):
        slope, reps = refs[-2:]
        by_rows = (((1,), (1,)), ((), ()))
        logits = (
            lax.dot_general(rows[:, :deep], near[...], by_rows, preferred_element_type=F32)
            + lax.dot_general(rows[:, deep:], across[...], by_rows, preferred_element_type=F32)
            + bias[...]
        )
        if wide % tile:
            lanes = pl.program_id(0) * tile + lax.broadcasted_iota(jnp.int32, logits.shape, 1)
            logits = jnp.where(lanes < wide, logits, -1.0)
        at = 0
        for b in range(2):
            for i, span in enumerate(spans):
                x = logits[at : at + span]
                length = lens[b * 2 * count + i]
                grown = 1.0 + jnp.maximum(x, 0.0)
                p2 = grown * grown
                p4 = p2 * p2
                p8 = p4 * p4
                valid = lax.broadcasted_iota(jnp.int32, (span, tile), 0) < length
                p19 = jnp.where(valid, p8 * p8 * (p2 * grown), 0.0)
                summed = jnp.sum(p19 * grown, axis=0, keepdims=True)
                rep = TAU * jnp.log(summed / length.astype(F32))
                reps[i // count, pl.ds(b * count + i % count, 1), :] = rep
                slope[0, at : at + span, :] = jnp.where(x > 0, p19, 0.0) * (1.0 / summed)
                at += span

    first = start // tile
    old = [] if slopes is None else [slopes]
    return pl.pallas_call(
        kernel,
        grid_spec=pltpu.PrefetchScalarGridSpec(
            num_scalar_prefetch=1,
            grid=(tiles,),
            in_specs=[
                pl.BlockSpec(memory_space=pltpu.VMEM),
                pl.BlockSpec((tile, deep), lambda c, lens: (c, 0)),
                pl.BlockSpec((tile, deep), lambda c, lens: (c, 0)),
                pl.BlockSpec((1, tile), lambda c, lens: (0, first + c)),
            ]
            + [pl.BlockSpec(memory_space=pl.ANY)] * len(old),
            out_specs=[
                pl.BlockSpec((1, tokens, tile), lambda c, lens: (first + c, 0, 0)),
                pl.BlockSpec((2, 2 * count, tile), lambda c, lens: (0, 0, c)),
            ],
        ),
        out_shape=[
            pltpu.HBM((bias.shape[1] // tile, tokens, tile), F32),
            jax.ShapeDtypeStruct((2, 2 * count, tiles * tile), F32),
        ],
        input_output_aliases={5: 0} if old else {},
        compiler_params=pltpu.CompilerParams(vmem_limit_bytes=40 * 2**20),
        cost_estimate=NO_COST,
        name=f"forward{start}",
    )(lens, in_vmem(rows), *in_hbm(near, across), bias, *in_hbm(*old))


def margins(parts, id_place, teachers, slopes, early, late):
    tiles, tokens, tile = slopes.shape
    queries, neg_count = teachers.shape
    pair = early.shape[1] // 8
    split_at = early.shape[2] // tile

    def kernel(s0, s1, s2, s3, ids, teach, slope, early, late, margin, grad, coeff, coeff_t):
        step = pl.program_id(0)

        @pl.when(step == 0)
        def _():
            score = (s0[...] + s1[...]) + (s2[...] + s3[...])
            lanes = lax.broadcasted_iota(jnp.int32, score.shape, 1)
            eye = lax.broadcasted_iota(jnp.int32, score.shape, 0) == lanes
            positive = jnp.sum(jnp.where(eye, score, 0.0), axis=1, keepdims=True)
            total = jnp.zeros_like(score)
            grad_pos = jnp.zeros_like(positive)
            for k in range(neg_count):
                chosen = ids[:, k : k + 1] == lanes
                negative = jnp.sum(jnp.where(chosen, score, 0.0), axis=1, keepdims=True)
                error = positive - negative - teach[:, k : k + 1]
                margin[:, k : k + 1] = error
                total = total - jnp.where(chosen, error, 0.0)
                grad_pos = grad_pos + error
            total = total + jnp.where(eye, grad_pos, 0.0)
            coeff[...] = total
            coeff_t[...] = total.T

        def fill(reps):
            grad_q = jnp.dot(coeff[:pair], reps[1], precision=HIGHEST, preferred_element_type=F32)
            grad_p = jnp.dot(coeff_t[:pair], reps[0], precision=HIGHEST, preferred_element_type=F32)
            at = 0
            for b in range(2):
                for span, part in ((LQ, grad_q), (LP, grad_p)):
                    for i in range(pair // 2):
                        row = b * (pair // 2) + i
                        grad[at : at + span, :] = (
                            slope[0, at : at + span, :] * part[row : row + 1]
                        ).astype(BF16)
                        at += span

        @pl.when(step < split_at)
        def _():
            fill(early)

        @pl.when(step >= split_at)
        def _():
            fill(late)

    square = pl.BlockSpec((queries, queries), lambda c: (0, 0))
    listed = pl.BlockSpec((queries, neg_count), lambda c: (0, 0))
    return pl.pallas_call(
        kernel,
        grid=(tiles,),
        in_specs=[square] * 4
        + [listed] * 2
        + [
            pl.BlockSpec((1, tokens, tile), lambda c: (c, 0, 0)),
            pl.BlockSpec((2, queries, tile), lambda c: (0, 0, jnp.minimum(c, split_at - 1))),
            pl.BlockSpec((2, queries, tile), lambda c: (0, 0, jnp.maximum(c - split_at, 0))),
        ],
        out_specs=[listed, pl.BlockSpec((tokens, tile), lambda c: (0, c))],
        out_shape=[
            jax.ShapeDtypeStruct((queries, neg_count), F32),
            pltpu.VMEM((tokens, tiles * tile), BF16),
        ],
        scratch_shapes=[pltpu.VMEM((queries, queries), F32)] * 2,
        compiler_params=pltpu.CompilerParams(vmem_limit_bytes=40 * 2**20),
        name="margins",
    )(*parts, id_place, teachers, *in_hbm(slopes), early, late)


def back_piece(place, grads, heads, piece, pieces):
    n = len(heads)
    rows, block = grads.shape[0], heads[0].shape[1] // 8
    steps = 16 // pieces
    half = rows // 4

    def kernel(place, grad, *refs):
        heads, (send_x, keep_x, send_z, keep_z, total) = refs[:n], refs[n:]
        sums, start = None, 0
        for head in heads:
            wide = head.shape[0]
            part = jnp.dot(grad[:, start : start + wide], head[...], preferred_element_type=F32)
            sums = part if sums is None else sums + part
            start += wide
        total[...] = sums
        zlo, x = place[0], place[1]

        def rows_of(z, x):
            return total[pl.ds((2 * z + x) * half, half), :]

        @pl.when(pl.program_id(0) < steps // 2)
        def _():
            keep_x[0], keep_x[1] = rows_of(zlo, x), rows_of(1 - zlo, x)
            send_x[0] = rows_of(zlo, 1 - x).astype(BF16)
            send_x[1] = rows_of(1 - zlo, 1 - x).astype(BF16)

        @pl.when(pl.program_id(0) >= steps // 2)
        def _():
            keep_z[0], keep_z[1] = rows_of(zlo, x), rows_of(zlo, 1 - x)
            send_z[0] = rows_of(1 - zlo, x).astype(BF16)
            send_z[1] = rows_of(1 - zlo, 1 - x).astype(BF16)

    some = [
        pl.BlockSpec((h.shape[0], block), lambda d, place: (0, piece % 2 * steps + d))
        for h in heads
    ]
    last = steps // 2 - 1
    by_x = pl.BlockSpec(
        (2, half, block), lambda d, place: (0, 0, jnp.minimum(d, last) ^ place[0])
    )
    by_z = pl.BlockSpec(
        (2, half, block), lambda d, place: (0, 0, jnp.maximum(d - last - 1, 0) ^ place[0])
    )
    shape = (2, half, steps // 2 * block)
    return pl.pallas_call(
        kernel,
        grid_spec=pltpu.PrefetchScalarGridSpec(
            num_scalar_prefetch=1,
            grid=(steps,),
            in_specs=[pl.BlockSpec(memory_space=pltpu.VMEM)] + some,
            out_specs=[by_x, by_x, by_z, by_z],
            scratch_shapes=[pltpu.VMEM((rows, block), F32)],
        ),
        out_shape=[pltpu.HBM(shape, t) for t in (BF16, F32, BF16, F32)],
        compiler_params=pltpu.CompilerParams(vmem_limit_bytes=40 * 2**20),
        cost_estimate=pl.CostEstimate(
            flops=2 * rows * grads.shape[1] * steps * block,
            bytes_accessed=2 * grads.shape[1] * steps * block + 3 * rows * steps * block,
            transcendentals=0,
        ),
        name=f"back{piece}",
    )(place, in_vmem(grads), *in_hbm(*heads))


def finish(places, pairs):
    count = len(pairs)
    rows, width = pairs[0][0].shape
    blocks = 16 // count
    block = width // blocks
    step = 32

    def kernel(places, *refs):
        out = refs[-1]
        for i in range(count):
            for k in range(blocks):
                cols = slice(k * block, (k + 1) * block)
                lanes = pl.ds(pl.multiple_of(places[i * blocks + k] * block, block), block)
                out[:, lanes] = refs[2 * i][:, cols] + refs[2 * i + 1][:, cols].astype(F32)

    return pl.pallas_call(
        kernel,
        grid_spec=pltpu.PrefetchScalarGridSpec(
            num_scalar_prefetch=1,
            grid=(rows // step,),
            in_specs=[pl.BlockSpec((step, width), lambda r, places: (r, 0))] * (2 * count),
            out_specs=pl.BlockSpec((step, 16 * block), lambda r, places: (r, 0)),
        ),
        out_shape=jax.ShapeDtypeStruct((rows, 16 * block), F32),
        compiler_params=pltpu.CompilerParams(vmem_limit_bytes=40 * 2**20),
        name="finish",
    )(places, *[a for pair in pairs for a in pair])


def by_squares(
    hidden, head_weight, head_bias, query_len, passage_len, neg_owner, neg_index, teacher
):
    count, neg_count = neg_owner.shape
    tokens, width = hidden.shape
    depth, columns = head_weight.shape
    share = columns // 2
    padded = -(-share // 256) * 256
    n = len(CHUNKS)
    starts = [sum(CHUNKS[:j]) for j in range(n)]
    me = lax.axis_index("dp")
    x = lax.axis_index("vocab")
    zlo = (me >> 2) & 1
    place = jnp.stack([zlo, x]).astype(jnp.int32)
    blocks = me ^ jnp.array(ORDER, jnp.int32)
    head = head_weight.T
    bias = jnp.pad(
        lax.dynamic_slice(head_bias, (zlo * share,), (share,)),
        (0, padded - share),
        constant_values=-1.0,
    )[None, :]
    half, piece = tokens // 2, tokens // 2 // len(HIDDEN)

    live = {}

    def columns_of(chunks, low):
        first, size = starts[chunks[0]], sum(CHUNKS[c] for c in chunks)
        return lax.dynamic_slice(head, (low * share + first, 0), (size, depth))

    for k, chunks in NEAR.items():
        live["given", k] = columns_of(chunks, 1 - zlo)
    for i, k in enumerate(HIDDEN):
        live["hidden", k] = lax.dynamic_slice(hidden, (x * half + i * piece, 0), (piece, width))
    table = jnp.concatenate(
        [
            (neg_owner * count + neg_index).astype(F32),
            teacher,
            query_len[:, None].astype(F32),
            passage_len[:, None].astype(F32),
        ],
        axis=1,
    )

    def near_of(j):
        for k, chunks in NEAR.items():
            if j in chunks:
                first = starts[j] - starts[chunks[0]]
                return live["near", k][first : first + CHUNKS[j]]

    def beside(j):
        return jnp.concatenate([columns_of((j,), zlo), near_of(j)], axis=1)

    def all_reps(own, bits):
        return jnp.concatenate([own, swap(own, bits)], axis=1)

    rows = lens = slopes = None
    rounds = max(COMPUTED)
    for k in range(rounds + 1):
        sent = {}
        if 0 <= k - 1 < n:
            j = k - 1
            if ("two", j) not in live:
                live["two", j] = beside(j)
            sent["far", j] = swap(live["two", j], ZHI)
            sent["side", j] = swap(live["two", j], Y)
        if 0 <= k - 2 < n:
            sent["beyond", k - 2] = swap(live["far", k - 2], Y)
        if k in NEAR:
            sent["near", k] = swap(live["given", k], ZLO)
        if k in HIDDEN:
            sent["from_z", k] = swap(live["hidden", k], ZLO)
        if k - 1 in HIDDEN:
            sent["from_x", k - 1] = swap(live["from_z", k - 1], X)
        for g in range(len(GROUPS)):
            if k == PACKED[g]:
                sent["quads", g] = pack(
                    [[live[name, j] for name in ("two", "far", "side", "beyond")] for j in GROUPS[g]]
                )
            if k == MOVED[g]:
                quads = sent if k == PACKED[g] else live
                sent["across", g] = swap(quads["quads", g], CORE)
        if k in TABLE:
            came = swap(table, TABLE[k])
            both = [table, came]
            if TABLE[k] == ZLO:
                both = [jnp.where(zlo == 0, table, came), jnp.where(zlo == 0, came, table)]
            sent["table"] = jnp.concatenate(both)
        if k == max(HIDDEN) + 2:
            by_z, by_x = (
                jnp.concatenate([live[name, i] for i in HIDDEN]) for name in ("from_z", "from_x")
            )
            other = jnp.concatenate(
                [jnp.where(x == 0, by_z, by_x), jnp.where(x == 0, by_x, by_z)]
            )
            rows = arrange(blocks, hidden, other)
            pair_lens = table[: 2 * count, 2 * neg_count :].astype(jnp.int32)
            lens = pair_lens.reshape(2, count, 2).transpose(0, 2, 1).reshape(-1)
        for g in range(len(GROUPS)):
            if k == COMPUTED[g]:
                first = starts[GROUPS[g][0]]
                slopes, sent["reps", g] = forward(
                    lens, rows, live["quads", g], live["across", g], bias, slopes, first
                )
        if k in EARLY:
            own = live.get("early")
            if own is None:
                own = jnp.concatenate([live["reps", g] for g in range(EARLY_GROUPS)], axis=2)
            sent["early"] = all_reps(own, EARLY[k])
        live.update(sent)
        if k == rounds:
            break
        held = list(sent)
        if any(k in chunks[1:] for chunks in NEAR.values()):
            live["two", k] = beside(k)
            held.append(("two", k))
        held += [key for key in (("given", k + 1), ("hidden", k + 1)) if key in live]
        live.update(zip(held, lax.optimization_barrier([live[key] for key in held])))
        table = live["table"]
    ids = table[:, :neg_count].astype(jnp.int32)
    teachers = table[:, neg_count : 2 * neg_count]
    owner = ids // count
    order = jnp.array(ORDER[::2], jnp.int32)
    group = jnp.sum(
        jnp.where(((owner ^ me) & ~4)[:, :, None] == order, jnp.arange(8, dtype=jnp.int32), 0),
        axis=2,
    )
    id_place = (group * 2 + ((owner >> 2) & 1)) * count + ids % count

    early = live["early"]
    late = jnp.concatenate([live["reps", g] for g in range(EARLY_GROUPS, len(GROUPS))], axis=2)
    for bits in (ZHI, Y, CORE):
        late = all_reps(late, bits)

    def scores(reps):
        return lax.dot_general(reps[0], reps[1], (((1,), (1,)), ((), ())), precision=HIGHEST)

    part = scores(early) + scores(late)
    margin_error, grads = margins(
        (part, swap(part, X), swap(part, ZLO), swap(part, ZLO | X)),
        id_place,
        teachers,
        slopes,
        early,
        late,
    )

    pieces = 4
    pairs, first = [], [None] * pieces

    def second(i):
        (keep_x, came_x), (keep_z, came_z) = first[i]
        mids = [
            (keep[1] + came[1].astype(F32)).astype(BF16)
            for keep, came in ((keep_x, came_x), (keep_z, came_z))
        ]
        nonlocal grads
        mid_x, mid_z, grads = lax.optimization_barrier((*mids, grads))
        pairs.append((keep_x[0] + came_x[0].astype(F32), swap(mid_x, ZLO)))
        pairs.append((keep_z[0] + came_z[0].astype(F32), swap(mid_z, X)))

    for i in range(pieces):
        heads = [live["quads" if i < 2 else "across", g] for g in range(len(GROUPS))]
        outs = back_piece(place, grads, heads, i, pieces)
        send_x, keep_x, send_z, keep_z, grads = lax.optimization_barrier((*outs, grads))
        first[i] = ((keep_x, swap(send_x, X)), (keep_z, swap(send_z, ZLO)))
        if i >= 1:
            second(i - 1)
    second(pieces - 1)
    places = []
    for k in range(0, 16, 2):
        base = (me & ~4) ^ ORDER[k]
        places += [base, base | 4]
    hidden_grad = finish(jnp.stack(places).astype(jnp.int32), pairs)
    return (lax.dynamic_slice(margin_error, (zlo * count, 0), (count, neg_count)), hidden_grad)


def solution(mesh):
    square = mesh.shape["dp"] == 16 and mesh.shape["vocab"] == 2
    return jax.shard_map(
        by_squares if square else any_mesh,
        mesh=mesh,
        in_specs=(
            P("dp", None),
            P("dp", "vocab"),
            P("vocab"),
            P("dp"),
            P("dp"),
            P("dp", None),
            P("dp", None),
            P("dp", None),
        ),
        out_specs=(P("dp", None), P(("dp", "vocab"), None)),
        check_vma=False,
    )
```

```python
import jax
import jax.numpy as jnp
from jax import lax
from jax.experimental import pallas as pl
from jax.experimental.pallas import tpu as pltpu
from jax.sharding import PartitionSpec as P

LQ = 32
LP = 64


TAU = 0.05
AXES = ("dp", "vocab")
F32 = jnp.float32
BF16 = jnp.bfloat16
X, CORE, Y, ZLO, ZHI = 1, 2, 4, 8, 16
ORDER = (0, 4, 8, 12, 2, 6, 10, 14, 1, 5, 9, 13, 3, 7, 11, 15)
CHUNKS = (256,) + (512,) * 7 + (160,)
NEAR = {0: (0,), 1: (1, 2), 3: (3, 4), 5: (5, 6), 7: (7, 8)}
HIDDEN = (2, 4)
TABLE = {1: ZLO, 2: ZHI, 10: Y, 11: CORE}
GROUPS = ((0,), (1, 2), (3,), (4,), (5,), (6,), (7,), (8,))
PACKED = (3, 5, 6, 7, 8, 9, 10, 11)
MOVED = (4, 6, 7, 8, 8, 9, 10, 11)
COMPUTED = (6, 7, 7, 8, 8, 9, 10, 11)
GATHERED = (((0, 1, 2), 9), ((3, 4, 5), 10), ((6, 7), None))
HIGHEST = lax.Precision.HIGHEST
NO_COST = pl.CostEstimate(flops=0, bytes_accessed=0, transcendentals=0)


def soft_pool(token_logits, token_mask):
    activation = jnp.log1p(jnp.maximum(token_logits, 0.0))
    weights = jnp.exp(activation / TAU) * token_mask[:, :, None]
    summed = jnp.sum(weights, axis=1)
    valid_count = jnp.sum(token_mask, axis=1)[:, None]
    return (TAU * jnp.log(summed / valid_count), weights / summed[:, None, :])


def lengths_mask(lengths, span):
    return (jnp.arange(span)[None, :] < lengths[:, None]).astype(jnp.float32)


def any_mesh(
    hidden, head_weight, head_bias, query_len, passage_len, neg_owner, neg_index, teacher
):
    query_count = neg_owner.shape[0]
    neg_count = neg_owner.shape[1]
    owners = lax.axis_size("dp")
    head_full = lax.all_gather(head_weight, "dp", axis=0, tiled=True)
    vocab_width = head_full.shape[1]
    logits = jnp.dot(hidden, head_full, preferred_element_type=jnp.float32) + head_bias[None, :]
    query_tokens = query_count * LQ
    query_rep, query_weights = soft_pool(
        logits[:query_tokens].reshape(query_count, LQ, vocab_width), lengths_mask(query_len, LQ)
    )
    passage_rep, passage_weights = soft_pool(
        logits[query_tokens:].reshape(query_count, LP, vocab_width), lengths_mask(passage_len, LP)
    )
    gathered = lax.all_gather(passage_rep, "dp", axis=0, tiled=True)
    passage_ids = neg_owner * query_count + neg_index
    neg_rows = jnp.take(gathered, passage_ids.reshape(-1), axis=0).reshape(
        query_count, neg_count, vocab_width
    )
    pos_part = jnp.sum(query_rep * passage_rep, axis=1)
    neg_part = jnp.sum(query_rep[:, None, :] * neg_rows, axis=2)
    positive, negative = lax.psum((pos_part, neg_part), "vocab")
    margin_error = positive[:, None] - negative - teacher
    grad_pos = jnp.sum(margin_error, axis=1)
    grad_neg = -margin_error
    query_grad = grad_pos[:, None] * passage_rep + jnp.sum(grad_neg[:, :, None] * neg_rows, axis=1)
    neg_terms = (grad_neg[:, :, None] * query_rep[:, None, :]).reshape(-1, vocab_width)
    scattered = jax.ops.segment_sum(
        neg_terms, passage_ids.reshape(-1), num_segments=owners * query_count
    )
    returned_grad = lax.psum_scatter(scattered, "dp", scatter_dimension=0, tiled=True)
    passage_grad = grad_pos[:, None] * query_rep + returned_grad
    relu_slope = (logits > 0).astype(jnp.float32) / (1.0 + jnp.maximum(logits, 0.0))
    d_query = (query_grad[:, None, :] * query_weights).reshape(-1, vocab_width)
    d_passage = (passage_grad[:, None, :] * passage_weights).reshape(-1, vocab_width)
    logit_grad = (jnp.concatenate([d_query, d_passage], axis=0) * relu_slope).astype(jnp.bfloat16)
    hidden_grad = lax.psum_scatter(
        lax.dot_general(
            logit_grad, head_full, (((1,), (1,)), ((), ())), preferred_element_type=jnp.float32
        ),
        "vocab",
        scatter_dimension=0,
        tiled=True,
    )
    return (margin_error, hidden_grad)


def in_hbm(*arrays):
    return [pltpu.with_memory_space_constraint(a, pltpu.HBM) for a in arrays]


def in_vmem(array):
    return pltpu.with_memory_space_constraint(array, pltpu.VMEM)


def swap(array, bits):
    return lax.ppermute(array, AXES, [(i, i ^ bits) for i in range(32)])


def arrange(places, x, hidden, by_z, by_x):
    rows, width = hidden.shape
    block = width // 16
    pieces = [*by_z, *by_x]
    step = pieces[0].shape[0]
    n = rows // step

    def kernel(places, hidden, *refs):
        sources, out = refs[:-1], refs[-1]

        def put(source):
            for k in range(16):
                lanes = pl.ds(pl.multiple_of(places[k] * block, block), block)
                out[:, k * block : (k + 1) * block] = source[:, lanes]

        at = pl.program_id(0)

        @pl.when(at < n)
        def _():
            put(hidden)

        for i, source in enumerate(sources):

            @pl.when(at == n + i)
            def _():
                put(source)

    def there(i, places):
        own = places[0] // 4 % 2
        piece = jnp.maximum(i - n, 0)
        half = (piece // len(by_z) + places[16]) % 2
        other = (1 - own) * n + half * len(by_z) + piece % len(by_z)
        return jnp.where(i < n, own * n + i, other), 0

    return pl.pallas_call(
        kernel,
        grid_spec=pltpu.PrefetchScalarGridSpec(
            num_scalar_prefetch=1,
            grid=(2 * n,),
            in_specs=[pl.BlockSpec((step, width), lambda i, places: (jnp.minimum(i, n - 1), 0))]
            + [pl.BlockSpec((step, width), lambda i, places: (0, 0))] * len(pieces),
            out_specs=pl.BlockSpec((step, width), there),
        ),
        out_shape=pltpu.VMEM((2 * rows, width), hidden.dtype),
        compiler_params=pltpu.CompilerParams(vmem_limit_bytes=24 * 2**20),
        cost_estimate=NO_COST,
        name="arrange",
    )(jnp.concatenate([places, x[None]]).astype(jnp.int32), hidden, *pieces)


def pack(groups):
    n = len(groups)
    block = groups[0][0].shape[1] // 2
    heights = [group[0].shape[0] for group in groups]
    step = 256 if all(h % 256 == 0 for h in heights) else heights[0]
    ends = [sum(heights[: i + 1]) // step for i in range(n)]
    firsts = [0] + ends[:-1]

    def kernel(*refs):
        out = refs[-1]
        for i in range(n):

            @pl.when((pl.program_id(0) >= firsts[i]) & (pl.program_id(0) < ends[i]))
            def _():
                for k in range(8):
                    out[k] = refs[4 * i + k // 2][:, k % 2 * block : (k % 2 + 1) * block]

    specs = []
    for i in range(n):
        last = heights[i] // step - 1
        specs += [
            pl.BlockSpec(
                (step, 2 * block), lambda r, i=i, last=last: (jnp.clip(r - firsts[i], 0, last), 0)
            )
        ] * 4
    return pl.pallas_call(
        kernel,
        grid=(ends[-1],),
        in_specs=specs,
        out_specs=pl.BlockSpec((8, step, block), lambda r: (0, r, 0)),
        out_shape=pltpu.HBM((8, sum(heights), block), BF16),
        compiler_params=pltpu.CompilerParams(vmem_limit_bytes=24 * 2**20),
        cost_estimate=NO_COST,
        name="pack",
    )(*in_hbm(*[a for group in groups for a in group]))


def forward(lens, rows, near, across, bias, slopes, start):
    tokens, depth = rows.shape
    blocks, wide, block = near.shape
    tile = 256
    tiles = -(-wide // tile)
    count = lens.shape[0] // 4
    spans = [LQ] * count + [LP] * count

    def kernel(lens, rows, near, across, bias, *refs):
        slope, reps = refs[-2:]
        by_rows = (((1,), (1,)), ((), ()))
        logits = bias[...]
        for k in range(2 * blocks):
            head = (near if k < blocks else across)[k % blocks]
            logits = logits + lax.dot_general(
                rows[:, k * block : (k + 1) * block], head, by_rows, preferred_element_type=F32
            )
        if wide % tile:
            lanes = pl.program_id(0) * tile + lax.broadcasted_iota(jnp.int32, logits.shape, 1)
            logits = jnp.where(lanes < wide, logits, -1.0)
        at = 0
        for b in range(2):
            for i, span in enumerate(spans):
                x = logits[at : at + span]
                length = lens[b * 2 * count + i]
                grown = 1.0 + jnp.maximum(x, 0.0)
                p2 = grown * grown
                p4 = p2 * p2
                p8 = p4 * p4
                valid = lax.broadcasted_iota(jnp.int32, (span, tile), 0) < length
                p19 = jnp.where(valid, p8 * p8 * (p2 * grown), 0.0)
                summed = jnp.sum(p19 * grown, axis=0, keepdims=True)
                rep = TAU * jnp.log(summed / length.astype(F32))
                reps[i // count, pl.ds(b * count + i % count, 1), :] = rep
                slope[0, at : at + span, :] = jnp.where(x > 0, p19, 0.0) * (1.0 / summed)
                at += span

    first = start // tile
    old = [] if slopes is None else [slopes]
    return pl.pallas_call(
        kernel,
        grid_spec=pltpu.PrefetchScalarGridSpec(
            num_scalar_prefetch=1,
            grid=(tiles,),
            in_specs=[
                pl.BlockSpec(memory_space=pltpu.VMEM),
                pl.BlockSpec((blocks, tile, block), lambda c, lens: (0, c, 0)),
                pl.BlockSpec((blocks, tile, block), lambda c, lens: (0, c, 0)),
                pl.BlockSpec((1, tile), lambda c, lens: (0, first + c)),
            ]
            + [pl.BlockSpec(memory_space=pl.ANY)] * len(old),
            out_specs=[
                pl.BlockSpec((1, tokens, tile), lambda c, lens: (first + c, 0, 0)),
                pl.BlockSpec((2, 2 * count, tile), lambda c, lens: (0, 0, c)),
            ],
        ),
        out_shape=[
            pltpu.HBM((bias.shape[1] // tile, tokens, tile), F32),
            jax.ShapeDtypeStruct((2, 2 * count, tiles * tile), F32),
        ],
        input_output_aliases={5: 0} if old else {},
        compiler_params=pltpu.CompilerParams(vmem_limit_bytes=24 * 2**20),
        cost_estimate=NO_COST,
        name=f"forward{start}",
    )(lens, in_vmem(rows), *in_hbm(near), across, bias, *in_hbm(*old))


def margins(parts, id_place, teachers, slopes, gathered):
    tiles, tokens, tile = slopes.shape
    queries, neg_count = teachers.shape
    pair = queries // 8
    n = len(gathered)
    ends = [sum(reps.shape[2] for reps in gathered[: i + 1]) // tile for i in range(n)]
    firsts = [0] + ends[:-1]
    batch = 4

    def kernel(s0, s1, s2, s3, ids, teach, slope, *refs):
        gathered, (margin, grad, coeff, coeff_t) = refs[:n], refs[n:]
        step = pl.program_id(0)

        @pl.when(step == 0)
        def _():
            score = (s0[...] + s1[...]) + (s2[...] + s3[...])
            lanes = lax.broadcasted_iota(jnp.int32, score.shape, 1)
            eye = lax.broadcasted_iota(jnp.int32, score.shape, 0) == lanes
            positive = jnp.sum(jnp.where(eye, score, 0.0), axis=1, keepdims=True)
            total = jnp.zeros_like(score)
            grad_pos = jnp.zeros_like(positive)
            for k in range(neg_count):
                chosen = ids[:, k : k + 1] == lanes
                negative = jnp.sum(jnp.where(chosen, score, 0.0), axis=1, keepdims=True)
                error = positive - negative - teach[:, k : k + 1]
                margin[:, k : k + 1] = error
                total = total - jnp.where(chosen, error, 0.0)
                grad_pos = grad_pos + error
            total = total + jnp.where(eye, grad_pos, 0.0)
            coeff[...] = total
            coeff_t[...] = total.T

        def fill(t, reps, first):
            there = pl.ds(pl.multiple_of((step * batch + t - first) * tile, tile), tile)
            here = pl.ds(pl.multiple_of((step * batch + t) * tile, tile), tile)
            grad_q = jnp.dot(
                coeff[:pair], reps[1, :, there], precision=HIGHEST, preferred_element_type=F32
            )
            grad_p = jnp.dot(
                coeff_t[:pair], reps[0, :, there], precision=HIGHEST, preferred_element_type=F32
            )
            at = 0
            for b in range(2):
                for span, part in ((LQ, grad_q), (LP, grad_p)):
                    for i in range(pair // 2):
                        row = b * (pair // 2) + i
                        grad[at : at + span, here] = (
                            slope[t, at : at + span, :] * part[row : row + 1]
                        ).astype(BF16)
                        at += span

        for t in range(batch):
            for reps, first, end in zip(gathered, firsts, ends):

                @pl.when((step * batch + t >= first) & (step * batch + t < end))
                def _():
                    fill(t, reps, first)

    square = pl.BlockSpec((queries, queries), lambda c: (0, 0))
    listed = pl.BlockSpec((queries, neg_count), lambda c: (0, 0))
    return pl.pallas_call(
        kernel,
        grid=(tiles // batch,),
        in_specs=[square] * 4
        + [listed] * 2
        + [pl.BlockSpec((batch, tokens, tile), lambda c: (c, 0, 0))]
        + [pl.BlockSpec(memory_space=pltpu.VMEM)] * n,
        out_specs=[listed, pl.BlockSpec(memory_space=pltpu.VMEM)],
        out_shape=[
            jax.ShapeDtypeStruct((queries, neg_count), F32),
            pltpu.VMEM((tokens, tiles * tile), BF16),
        ],
        scratch_shapes=[pltpu.VMEM((queries, queries), F32)] * 2,
        compiler_params=pltpu.CompilerParams(vmem_limit_bytes=24 * 2**20),
        name="margins",
    )(*parts, id_place, teachers, *in_hbm(slopes), *gathered)


def back_piece(place, grads, heads, piece, pieces):
    n = len(heads)
    rows, block = grads.shape[0], heads[0].shape[2]
    steps = 16 // pieces
    half = rows // 4

    def kernel(place, grad, *refs):
        heads, (send_x, keep_x, send_z, keep_z, total) = refs[:n], refs[n:]
        sums, start = None, 0
        for head in heads:
            wide = head.shape[1]
            part = jnp.dot(grad[:, start : start + wide], head[0], preferred_element_type=F32)
            sums = part if sums is None else sums + part
            start += wide
        total[...] = sums
        zlo, x = place[0], place[1]

        def rows_of(z, x):
            return total[pl.ds((2 * z + x) * half, half), :]

        @pl.when(pl.program_id(0) < steps // 2)
        def _():
            keep_x[0], keep_x[1] = rows_of(zlo, x), rows_of(1 - zlo, x)
            send_x[0] = rows_of(zlo, 1 - x).astype(BF16)
            send_x[1] = rows_of(1 - zlo, 1 - x).astype(BF16)

        @pl.when(pl.program_id(0) >= steps // 2)
        def _():
            keep_z[0], keep_z[1] = rows_of(zlo, x), rows_of(zlo, 1 - x)
            send_z[0] = rows_of(1 - zlo, x).astype(BF16)
            send_z[1] = rows_of(1 - zlo, 1 - x).astype(BF16)

    some = [
        pl.BlockSpec((1, h.shape[1], block), lambda d, place: (piece % 2 * steps + d, 0, 0))
        for h in heads
    ]
    last = steps // 2 - 1
    by_x = pl.BlockSpec(
        (2, half, block), lambda d, place: (0, 0, jnp.minimum(d, last) ^ place[0])
    )
    by_z = pl.BlockSpec(
        (2, half, block), lambda d, place: (0, 0, jnp.maximum(d - last - 1, 0) ^ place[0])
    )
    shape = (2, half, steps // 2 * block)
    return pl.pallas_call(
        kernel,
        grid_spec=pltpu.PrefetchScalarGridSpec(
            num_scalar_prefetch=1,
            grid=(steps,),
            in_specs=[pl.BlockSpec(memory_space=pltpu.VMEM)] + some,
            out_specs=[by_x, by_x, by_z, by_z],
            scratch_shapes=[pltpu.VMEM((rows, block), F32)],
        ),
        out_shape=[pltpu.HBM(shape, t) for t in (BF16, F32, BF16, F32)],
        compiler_params=pltpu.CompilerParams(vmem_limit_bytes=24 * 2**20),
        cost_estimate=pl.CostEstimate(
            flops=2 * rows * grads.shape[1] * steps * block,
            bytes_accessed=2 * grads.shape[1] * steps * block + 3 * rows * steps * block,
            transcendentals=0,
        ),
        name=f"back{piece}",
    )(place, in_vmem(grads), *in_hbm(*heads))


def finish(places, pairs):
    count = len(pairs)
    rows, width = pairs[0][0].shape
    blocks = 16 // count
    block = width // blocks
    step = rows // 2

    def kernel(places, *refs):
        out = refs[-1]
        for i in range(count):
            for k in range(blocks):
                cols = slice(k * block, (k + 1) * block)
                lanes = pl.ds(pl.multiple_of(places[i * blocks + k] * block, block), block)
                out[:, lanes] = refs[2 * i][:, cols] + refs[2 * i + 1][:, cols].astype(F32)

    return pl.pallas_call(
        kernel,
        grid_spec=pltpu.PrefetchScalarGridSpec(
            num_scalar_prefetch=1,
            grid=(rows // step,),
            in_specs=[pl.BlockSpec((step, width), lambda r, places: (r, 0))] * (2 * count),
            out_specs=pl.BlockSpec((step, 16 * block), lambda r, places: (r, 0)),
        ),
        out_shape=jax.ShapeDtypeStruct((rows, 16 * block), F32),
        compiler_params=pltpu.CompilerParams(vmem_limit_bytes=24 * 2**20),
        name="finish",
    )(places, *[a for pair in pairs for a in pair])


def by_squares(
    hidden, head_weight, head_bias, query_len, passage_len, neg_owner, neg_index, teacher
):
    count, neg_count = neg_owner.shape
    tokens, width = hidden.shape
    depth, columns = head_weight.shape
    share = columns // 2
    padded = -(-share // 256) * 256
    n = len(CHUNKS)
    starts = [sum(CHUNKS[:j]) for j in range(n)]
    me = lax.axis_index("dp")
    x = lax.axis_index("vocab")
    zlo = (me >> 2) & 1
    place = jnp.stack([zlo, x]).astype(jnp.int32)
    blocks = me ^ jnp.array(ORDER, jnp.int32)
    head = head_weight.T
    bias = jnp.pad(
        lax.dynamic_slice(head_bias, (zlo * share,), (share,)),
        (0, padded - share),
        constant_values=-1.0,
    )[None, :]
    half, piece = tokens // 2, tokens // 2 // len(HIDDEN)

    live = {}

    def columns_of(chunks, low):
        first, size = starts[chunks[0]], sum(CHUNKS[c] for c in chunks)
        return jnp.where(
            low == 0, head[first : first + size], head[share + first : share + first + size]
        )

    for k, chunks in NEAR.items():
        live["given", k] = columns_of(chunks, 1 - zlo)
    for i, k in enumerate(HIDDEN):
        live["hidden", k] = lax.dynamic_slice(hidden, (x * half + i * piece, 0), (piece, width))
    live["table"] = jnp.concatenate(
        [
            (neg_owner * count + neg_index).astype(F32),
            teacher,
            query_len[:, None].astype(F32),
            passage_len[:, None].astype(F32),
        ],
        axis=1,
    )

    def near_of(j):
        for k, chunks in NEAR.items():
            if j in chunks:
                first = starts[j] - starts[chunks[0]]
                return live["near", k][first : first + CHUNKS[j]]

    def beside(j):
        return jnp.concatenate([columns_of((j,), zlo), near_of(j)], axis=1)

    def reps_of(groups):
        return jnp.concatenate([live["reps", g] for g in groups], axis=2)

    rows = lens = slopes = None
    rounds = max(COMPUTED) + 2
    for k in range(rounds + 1):
        sent = {}
        if 0 <= k - 1 < n:
            j = k - 1
            if ("two", j) not in live:
                live["two", j] = beside(j)
            sent["far", j] = swap(live["two", j], ZHI)
            sent["side", j] = swap(live["two", j], Y)
        if 0 <= k - 2 < n:
            sent["beyond", k - 2] = swap(live["far", k - 2], Y)
        for i in NEAR:
            if k == max(i - (i == 1), 0):
                sent["near", i] = swap(live["given", i], ZLO)
        if k in HIDDEN:
            sent["from_z", k] = swap(live["hidden", k], ZLO)
        if k - 1 in HIDDEN:
            sent["from_x", k - 1] = swap(live["from_z", k - 1], X)
        if k - 1 in TABLE:
            table, came = live["table"], live["table came"]
            both = [table, came]
            if TABLE[k - 1] == ZLO:
                both = [jnp.where(zlo == 0, table, came), jnp.where(zlo == 0, came, table)]
            live["table"] = jnp.concatenate(both)
        if k in TABLE:
            sent["table came"] = swap(live["table"], TABLE[k])
        if k == max(HIDDEN) + 2:
            by_z, by_x = ([live[name, i] for i in HIDDEN] for name in ("from_z", "from_x"))
            rows = arrange(blocks, x, hidden, by_z, by_x)
            pair_lens = live["table"][: 2 * count, 2 * neg_count :].astype(jnp.int32)
            lens = pair_lens.reshape(2, count, 2).transpose(0, 2, 1).reshape(-1)
        for g in range(len(GROUPS)):
            if k == PACKED[g]:
                arrays = [live[name, j] for j in GROUPS[g] for name in ("two", "far", "side", "beyond")]
                sent["quads", g] = pack([arrays[4 * i : 4 * i + 4] for i in range(len(GROUPS[g]))])
            if k == MOVED[g]:
                quads = sent if k == PACKED[g] else live
                sent["across", g] = swap(quads["quads", g], CORE)
            if k == COMPUTED[g]:
                first = starts[GROUPS[g][0]]
                quads, across = (
                    sent[key] if key in sent else live[key] for key in (("quads", g), ("across", g))
                )
                slopes, sent["reps", g] = forward(lens, rows, quads, across, bias, slopes, first)
        for groups, first in GATHERED:
            if first is None or not 0 <= k - first <= 3:
                continue
            if k == first:
                own = reps_of(groups)
            else:
                own = jnp.concatenate([live["gathered", groups], live["came", groups]], axis=1)
            live["gathered", groups] = own
            if k - first < 3:
                sent["came", groups] = swap(own, (ZHI, Y, CORE)[k - first])
        live.update(sent)
        if k > max(COMPUTED):
            continue
        held = list(sent)
        if k == 0:
            held.remove(("near", 1))
        if k == 1:
            held.append(("near", 1))
        if any(k in chunks[1:] for chunks in NEAR.values()):
            live["two", k] = beside(k)
            held.append(("two", k))
        held += [key for key in (("given", k + 1), ("hidden", k + 1)) if key in live]
        live.update(zip(held, lax.optimization_barrier([live[key] for key in held])))
    ids = live["table"][:, :neg_count].astype(jnp.int32)
    teachers = live["table"][:, neg_count : 2 * neg_count]
    owner = ids // count
    order = jnp.array(ORDER[::2], jnp.int32)
    group = jnp.sum(
        jnp.where(((owner ^ me) & ~4)[:, :, None] == order, jnp.arange(8, dtype=jnp.int32), 0),
        axis=2,
    )
    id_place = (group * 2 + ((owner >> 2) & 1)) * count + ids % count

    late = reps_of(GATHERED[-1][0])
    for bits in (ZHI, Y, CORE):
        late = jnp.concatenate([late, swap(late, bits)], axis=1)
    gathered = [live["gathered", groups] for groups, _ in GATHERED[:-1]] + [late]

    def scores(reps):
        return lax.dot_general(reps[0], reps[1], (((1,), (1,)), ((), ())), precision=HIGHEST)

    part = sum(scores(reps) for reps in gathered)
    margin_error, grads = margins(
        (part, swap(part, X), swap(part, ZLO), swap(part, ZLO | X)),
        id_place,
        teachers,
        slopes,
        gathered,
    )

    pieces = 4
    pairs, first = [], [None] * pieces

    def second(i):
        (keep_x, came_x), (keep_z, came_z) = first[i]
        mids = [
            (keep[1] + came[1].astype(F32)).astype(BF16)
            for keep, came in ((keep_x, came_x), (keep_z, came_z))
        ]
        nonlocal grads
        mid_x, mid_z, grads = lax.optimization_barrier((*mids, grads))
        pairs.append((keep_x[0] + came_x[0].astype(F32), swap(mid_x, ZLO)))
        pairs.append((keep_z[0] + came_z[0].astype(F32), swap(mid_z, X)))

    for i in range(pieces):
        heads = [live["quads" if i < 2 else "across", g] for g in range(len(GROUPS))]
        outs = back_piece(place, grads, heads, i, pieces)
        send_x, keep_x, send_z, keep_z, grads = lax.optimization_barrier((*outs, grads))
        first[i] = ((keep_x, swap(send_x, X)), (keep_z, swap(send_z, ZLO)))
        if i >= 1:
            second(i - 1)
    second(pieces - 1)
    places = []
    for k in range(0, 16, 2):
        base = (me & ~4) ^ ORDER[k]
        places += [base, base | 4]
    hidden_grad = finish(jnp.stack(places).astype(jnp.int32), pairs)
    return (lax.dynamic_slice(margin_error, (zlo * count, 0), (count, neg_count)), hidden_grad)


def solution(mesh):
    square = mesh.shape["dp"] == 16 and mesh.shape["vocab"] == 2
    return jax.shard_map(
        by_squares if square else any_mesh,
        mesh=mesh,
        in_specs=(
            P("dp", None),
            P("dp", "vocab"),
            P("vocab"),
            P("dp"),
            P("dp"),
            P("dp", None),
            P("dp", None),
            P("dp", None),
        ),
        out_specs=(P("dp", None), P(("dp", "vocab"), None)),
        check_vma=False,
    )
```

```python
import jax
import jax.numpy as jnp
from jax import lax
from jax.experimental import pallas as pl
from jax.experimental.pallas import tpu as pltpu
from jax.sharding import PartitionSpec as P

LQ = 32
LP = 64


TAU = 0.05
AXES = ("dp", "vocab")
F32 = jnp.float32
BF16 = jnp.bfloat16
X, CORE, Y, ZLO, ZHI = 1, 2, 4, 8, 16
ORDER = (0, 4, 8, 12, 2, 6, 10, 14, 1, 5, 9, 13, 3, 7, 11, 15)
CHUNKS = (256,) + (512,) * 7 + (160,)
NEAR = {0: (0,), 1: (1, 2), 3: (3, 4), 5: (5, 6), 7: (7, 8)}
HIDDEN = (2, 4)
TABLE = {1: ZLO, 2: ZHI, 10: Y, 11: CORE}
GROUPS = ((0,), (1, 2), (3,), (4,), (5,), (6,), (7,), (8,))
PACKED = (3, 5, 6, 7, 8, 9, 10, 11)
MOVED = (4, 6, 7, 8, 8, 9, 10, 11)
COMPUTED = (6, 7, 7, 8, 8, 9, 10, 11)
GATHERED = (((0, 1, 2), 9), ((3, 4, 5), 10), ((6, 7), None))
PIECES = ((0, 8), (8, 4), (12, 4))
HIGHEST = lax.Precision.HIGHEST
NO_COST = pl.CostEstimate(flops=0, bytes_accessed=0, transcendentals=0)


def soft_pool(token_logits, token_mask):
    activation = jnp.log1p(jnp.maximum(token_logits, 0.0))
    weights = jnp.exp(activation / TAU) * token_mask[:, :, None]
    summed = jnp.sum(weights, axis=1)
    valid_count = jnp.sum(token_mask, axis=1)[:, None]
    return (TAU * jnp.log(summed / valid_count), weights / summed[:, None, :])


def lengths_mask(lengths, span):
    return (jnp.arange(span)[None, :] < lengths[:, None]).astype(jnp.float32)


def any_mesh(
    hidden, head_weight, head_bias, query_len, passage_len, neg_owner, neg_index, teacher
):
    query_count = neg_owner.shape[0]
    neg_count = neg_owner.shape[1]
    owners = lax.axis_size("dp")
    head_full = lax.all_gather(head_weight, "dp", axis=0, tiled=True)
    vocab_width = head_full.shape[1]
    logits = jnp.dot(hidden, head_full, preferred_element_type=jnp.float32) + head_bias[None, :]
    query_tokens = query_count * LQ
    query_rep, query_weights = soft_pool(
        logits[:query_tokens].reshape(query_count, LQ, vocab_width), lengths_mask(query_len, LQ)
    )
    passage_rep, passage_weights = soft_pool(
        logits[query_tokens:].reshape(query_count, LP, vocab_width), lengths_mask(passage_len, LP)
    )
    gathered = lax.all_gather(passage_rep, "dp", axis=0, tiled=True)
    passage_ids = neg_owner * query_count + neg_index
    neg_rows = jnp.take(gathered, passage_ids.reshape(-1), axis=0).reshape(
        query_count, neg_count, vocab_width
    )
    pos_part = jnp.sum(query_rep * passage_rep, axis=1)
    neg_part = jnp.sum(query_rep[:, None, :] * neg_rows, axis=2)
    positive, negative = lax.psum((pos_part, neg_part), "vocab")
    margin_error = positive[:, None] - negative - teacher
    grad_pos = jnp.sum(margin_error, axis=1)
    grad_neg = -margin_error
    query_grad = grad_pos[:, None] * passage_rep + jnp.sum(grad_neg[:, :, None] * neg_rows, axis=1)
    neg_terms = (grad_neg[:, :, None] * query_rep[:, None, :]).reshape(-1, vocab_width)
    scattered = jax.ops.segment_sum(
        neg_terms, passage_ids.reshape(-1), num_segments=owners * query_count
    )
    returned_grad = lax.psum_scatter(scattered, "dp", scatter_dimension=0, tiled=True)
    passage_grad = grad_pos[:, None] * query_rep + returned_grad
    relu_slope = (logits > 0).astype(jnp.float32) / (1.0 + jnp.maximum(logits, 0.0))
    d_query = (query_grad[:, None, :] * query_weights).reshape(-1, vocab_width)
    d_passage = (passage_grad[:, None, :] * passage_weights).reshape(-1, vocab_width)
    logit_grad = (jnp.concatenate([d_query, d_passage], axis=0) * relu_slope).astype(jnp.bfloat16)
    hidden_grad = lax.psum_scatter(
        lax.dot_general(
            logit_grad, head_full, (((1,), (1,)), ((), ())), preferred_element_type=jnp.float32
        ),
        "vocab",
        scatter_dimension=0,
        tiled=True,
    )
    return (margin_error, hidden_grad)


def in_hbm(*arrays):
    return [pltpu.with_memory_space_constraint(a, pltpu.HBM) for a in arrays]


def in_vmem(array):
    return pltpu.with_memory_space_constraint(array, pltpu.VMEM)


def swap(array, bits):
    return lax.ppermute(array, AXES, [(i, i ^ bits) for i in range(32)])


def arrange(places, x, hidden, by_z, by_x):
    rows, width = hidden.shape
    block = width // 16
    pieces = [*by_z, *by_x]
    step = pieces[0].shape[0]
    n = rows // step

    def kernel(places, hidden, *refs):
        sources, out = refs[:-1], refs[-1]

        def put(source):
            for k in range(16):
                lanes = pl.ds(pl.multiple_of(places[k] * block, block), block)
                out[:, k * block : (k + 1) * block] = source[:, lanes]

        at = pl.program_id(0)

        @pl.when(at < n)
        def _():
            put(hidden)

        for i, source in enumerate(sources):

            @pl.when(at == n + i)
            def _():
                put(source)

    def there(i, places):
        own = places[0] // 4 % 2
        piece = jnp.maximum(i - n, 0)
        half = (piece // len(by_z) + places[16]) % 2
        other = (1 - own) * n + half * len(by_z) + piece % len(by_z)
        return jnp.where(i < n, own * n + i, other), 0

    return pl.pallas_call(
        kernel,
        grid_spec=pltpu.PrefetchScalarGridSpec(
            num_scalar_prefetch=1,
            grid=(2 * n,),
            in_specs=[pl.BlockSpec((step, width), lambda i, places: (jnp.minimum(i, n - 1), 0))]
            + [pl.BlockSpec((step, width), lambda i, places: (0, 0))] * len(pieces),
            out_specs=pl.BlockSpec((step, width), there),
        ),
        out_shape=pltpu.VMEM((2 * rows, width), hidden.dtype),
        compiler_params=pltpu.CompilerParams(vmem_limit_bytes=24 * 2**20),
        cost_estimate=NO_COST,
        name="arrange",
    )(jnp.concatenate([places, x[None]]).astype(jnp.int32), hidden, *pieces)


def pack(groups):
    n = len(groups)
    block = groups[0][0].shape[1] // 2
    heights = [group[0].shape[0] for group in groups]
    step = 256 if all(h % 256 == 0 for h in heights) else heights[0]
    ends = [sum(heights[: i + 1]) // step for i in range(n)]
    firsts = [0] + ends[:-1]

    def kernel(*refs):
        out = refs[-1]
        for i in range(n):

            @pl.when((pl.program_id(0) >= firsts[i]) & (pl.program_id(0) < ends[i]))
            def _():
                for k in range(8):
                    out[k] = refs[4 * i + k // 2][:, k % 2 * block : (k % 2 + 1) * block]

    specs = []
    for i in range(n):
        last = heights[i] // step - 1
        specs += [
            pl.BlockSpec(
                (step, 2 * block), lambda r, i=i, last=last: (jnp.clip(r - firsts[i], 0, last), 0)
            )
        ] * 4
    return pl.pallas_call(
        kernel,
        grid=(ends[-1],),
        in_specs=specs,
        out_specs=pl.BlockSpec((8, step, block), lambda r: (0, r, 0)),
        out_shape=pltpu.HBM((8, sum(heights), block), BF16),
        compiler_params=pltpu.CompilerParams(vmem_limit_bytes=24 * 2**20),
        cost_estimate=NO_COST,
        name="pack",
    )(*in_hbm(*[a for group in groups for a in group]))


def forward(lens, rows, near, across, bias, slopes, start):
    tokens, depth = rows.shape
    blocks, wide, block = near.shape
    tile = 256
    tiles = -(-wide // tile)
    count = lens.shape[0] // 4
    spans = [LQ] * count + [LP] * count

    def kernel(lens, rows, near, across, bias, *refs):
        slope, reps = refs[-2:]
        by_rows = (((1,), (1,)), ((), ()))
        logits = bias[...]
        for k in range(2 * blocks):
            head = (near if k < blocks else across)[k % blocks]
            logits = logits + lax.dot_general(
                rows[:, k * block : (k + 1) * block], head, by_rows, preferred_element_type=F32
            )
        if wide % tile:
            lanes = pl.program_id(0) * tile + lax.broadcasted_iota(jnp.int32, logits.shape, 1)
            logits = jnp.where(lanes < wide, logits, -1.0)
        at = 0
        for b in range(2):
            for i, span in enumerate(spans):
                x = logits[at : at + span]
                length = lens[b * 2 * count + i]
                grown = 1.0 + jnp.maximum(x, 0.0)
                p2 = grown * grown
                p4 = p2 * p2
                p8 = p4 * p4
                valid = lax.broadcasted_iota(jnp.int32, (span, tile), 0) < length
                p19 = jnp.where(valid, p8 * p8 * (p2 * grown), 0.0)
                summed = jnp.sum(p19 * grown, axis=0, keepdims=True)
                rep = TAU * jnp.log(summed / length.astype(F32))
                reps[i // count, pl.ds(b * count + i % count, 1), :] = rep
                slope[0, at : at + span, :] = jnp.where(x > 0, p19, 0.0) * (1.0 / summed)
                at += span

    first = start // tile
    old = [] if slopes is None else [slopes]
    return pl.pallas_call(
        kernel,
        grid_spec=pltpu.PrefetchScalarGridSpec(
            num_scalar_prefetch=1,
            grid=(tiles,),
            in_specs=[
                pl.BlockSpec(memory_space=pltpu.VMEM),
                pl.BlockSpec((blocks, tile, block), lambda c, lens: (0, c, 0)),
                pl.BlockSpec((blocks, tile, block), lambda c, lens: (0, c, 0)),
                pl.BlockSpec((1, tile), lambda c, lens: (0, first + c)),
            ]
            + [pl.BlockSpec(memory_space=pl.ANY)] * len(old),
            out_specs=[
                pl.BlockSpec((1, tokens, tile), lambda c, lens: (first + c, 0, 0)),
                pl.BlockSpec((2, 2 * count, tile), lambda c, lens: (0, 0, c)),
            ],
        ),
        out_shape=[
            pltpu.HBM((bias.shape[1] // tile, tokens, tile), F32),
            jax.ShapeDtypeStruct((2, 2 * count, tiles * tile), F32),
        ],
        input_output_aliases={5: 0} if old else {},
        compiler_params=pltpu.CompilerParams(vmem_limit_bytes=24 * 2**20),
        cost_estimate=NO_COST,
        name=f"forward{start}",
    )(lens, in_vmem(rows), *in_hbm(near), across, bias, *in_hbm(*old))


def margins(parts, id_place, teachers, slopes, gathered):
    tiles, tokens, tile = slopes.shape
    queries, neg_count = teachers.shape
    pair = queries // 8
    n = len(gathered)
    ends = [sum(reps.shape[2] for reps in gathered[: i + 1]) // tile for i in range(n)]
    firsts = [0] + ends[:-1]
    batch = 4

    def kernel(s0, s1, s2, s3, ids, teach, slope, *refs):
        gathered, (margin, grad, coeff, coeff_t) = refs[:n], refs[n:]
        step = pl.program_id(0)

        @pl.when(step == 0)
        def _():
            score = (s0[...] + s1[...]) + (s2[...] + s3[...])
            lanes = lax.broadcasted_iota(jnp.int32, score.shape, 1)
            eye = lax.broadcasted_iota(jnp.int32, score.shape, 0) == lanes
            positive = jnp.sum(jnp.where(eye, score, 0.0), axis=1, keepdims=True)
            total = jnp.zeros_like(score)
            grad_pos = jnp.zeros_like(positive)
            for k in range(neg_count):
                chosen = ids[:, k : k + 1] == lanes
                negative = jnp.sum(jnp.where(chosen, score, 0.0), axis=1, keepdims=True)
                error = positive - negative - teach[:, k : k + 1]
                margin[:, k : k + 1] = error
                total = total - jnp.where(chosen, error, 0.0)
                grad_pos = grad_pos + error
            total = total + jnp.where(eye, grad_pos, 0.0)
            coeff[...] = total
            coeff_t[...] = total.T

        def fill(t, reps, first):
            there = pl.ds(pl.multiple_of((step * batch + t - first) * tile, tile), tile)
            here = pl.ds(pl.multiple_of((step * batch + t) * tile, tile), tile)
            grad_q = jnp.dot(
                coeff[:pair], reps[1, :, there], precision=HIGHEST, preferred_element_type=F32
            )
            grad_p = jnp.dot(
                coeff_t[:pair], reps[0, :, there], precision=HIGHEST, preferred_element_type=F32
            )
            at = 0
            for b in range(2):
                for span, part in ((LQ, grad_q), (LP, grad_p)):
                    for i in range(pair // 2):
                        row = b * (pair // 2) + i
                        grad[at : at + span, here] = (
                            slope[t, at : at + span, :] * part[row : row + 1]
                        ).astype(BF16)
                        at += span

        for t in range(batch):
            for reps, first, end in zip(gathered, firsts, ends):

                @pl.when((step * batch + t >= first) & (step * batch + t < end))
                def _():
                    fill(t, reps, first)

    square = pl.BlockSpec((queries, queries), lambda c: (0, 0))
    listed = pl.BlockSpec((queries, neg_count), lambda c: (0, 0))
    return pl.pallas_call(
        kernel,
        grid=(tiles // batch,),
        in_specs=[square] * 4
        + [listed] * 2
        + [pl.BlockSpec((batch, tokens, tile), lambda c: (c, 0, 0))]
        + [pl.BlockSpec(memory_space=pltpu.VMEM)] * n,
        out_specs=[listed, pl.BlockSpec(memory_space=pltpu.VMEM)],
        out_shape=[
            jax.ShapeDtypeStruct((queries, neg_count), F32),
            pltpu.VMEM((tokens, tiles * tile), BF16),
        ],
        scratch_shapes=[pltpu.VMEM((queries, queries), F32)] * 2,
        compiler_params=pltpu.CompilerParams(vmem_limit_bytes=24 * 2**20),
        name="margins",
    )(*parts, id_place, teachers, *in_hbm(slopes), *gathered)


def back_piece(place, grads, heads, begin, steps):
    n = len(heads)
    rows, block = grads.shape[0], heads[0].shape[2]
    half = rows // 4

    def kernel(place, grad, *refs):
        heads, (send_x, keep_x, send_z, keep_z, total) = refs[:n], refs[n:]
        sums, start = None, 0
        for head in heads:
            wide = head.shape[1]
            part = jnp.dot(grad[:, start : start + wide], head[0], preferred_element_type=F32)
            sums = part if sums is None else sums + part
            start += wide
        total[...] = sums
        zlo, x = place[0], place[1]

        def rows_of(z, x):
            return total[pl.ds((2 * z + x) * half, half), :]

        @pl.when(pl.program_id(0) < steps // 2)
        def _():
            keep_x[0], keep_x[1] = rows_of(zlo, x), rows_of(1 - zlo, x)
            send_x[0] = rows_of(zlo, 1 - x).astype(BF16)
            send_x[1] = rows_of(1 - zlo, 1 - x).astype(BF16)

        @pl.when(pl.program_id(0) >= steps // 2)
        def _():
            keep_z[0], keep_z[1] = rows_of(zlo, x), rows_of(zlo, 1 - x)
            send_z[0] = rows_of(1 - zlo, x).astype(BF16)
            send_z[1] = rows_of(1 - zlo, 1 - x).astype(BF16)

    some = [
        pl.BlockSpec((1, h.shape[1], block), lambda d, place: (begin % 8 + d, 0, 0))
        for h in heads
    ]
    last = steps // 2 - 1
    by_x = pl.BlockSpec(
        (2, half, block), lambda d, place: (0, 0, jnp.minimum(d, last) ^ place[0])
    )
    by_z = pl.BlockSpec(
        (2, half, block), lambda d, place: (0, 0, jnp.maximum(d - last - 1, 0) ^ place[0])
    )
    shape = (2, half, steps // 2 * block)
    return pl.pallas_call(
        kernel,
        grid_spec=pltpu.PrefetchScalarGridSpec(
            num_scalar_prefetch=1,
            grid=(steps,),
            in_specs=[pl.BlockSpec(memory_space=pltpu.VMEM)] + some,
            out_specs=[by_x, by_x, by_z, by_z],
            scratch_shapes=[pltpu.VMEM((rows, block), F32)],
        ),
        out_shape=[pltpu.HBM(shape, t) for t in (BF16, F32, BF16, F32)],
        compiler_params=pltpu.CompilerParams(vmem_limit_bytes=24 * 2**20),
        cost_estimate=pl.CostEstimate(
            flops=2 * rows * grads.shape[1] * steps * block,
            bytes_accessed=2 * grads.shape[1] * steps * block + 3 * rows * steps * block,
            transcendentals=0,
        ),
        name=f"back{begin}",
    )(place, in_vmem(grads), *in_hbm(*heads))


def finish(places, pairs):
    rows = pairs[0][0].shape[0]
    widths = [pair[0].shape[1] for pair in pairs]
    block = sum(widths) // 16
    step = rows // 2

    def kernel(places, *refs):
        out = refs[-1]
        at = 0
        for i, width in enumerate(widths):
            for k in range(width // block):
                cols = slice(k * block, (k + 1) * block)
                lanes = pl.ds(pl.multiple_of(places[at + k] * block, block), block)
                out[:, lanes] = refs[2 * i][:, cols] + refs[2 * i + 1][:, cols].astype(F32)
            at += width // block

    return pl.pallas_call(
        kernel,
        grid_spec=pltpu.PrefetchScalarGridSpec(
            num_scalar_prefetch=1,
            grid=(rows // step,),
            in_specs=[
                pl.BlockSpec((step, width), lambda r, places: (r, 0)) for width in widths for _ in range(2)
            ],
            out_specs=pl.BlockSpec((step, 16 * block), lambda r, places: (r, 0)),
        ),
        out_shape=jax.ShapeDtypeStruct((rows, 16 * block), F32),
        compiler_params=pltpu.CompilerParams(vmem_limit_bytes=24 * 2**20),
        name="finish",
    )(places, *[a for pair in pairs for a in pair])


def by_squares(
    hidden, head_weight, head_bias, query_len, passage_len, neg_owner, neg_index, teacher
):
    count, neg_count = neg_owner.shape
    tokens, width = hidden.shape
    depth, columns = head_weight.shape
    share = columns // 2
    padded = -(-share // 256) * 256
    n = len(CHUNKS)
    starts = [sum(CHUNKS[:j]) for j in range(n)]
    me = lax.axis_index("dp")
    x = lax.axis_index("vocab")
    zlo = (me >> 2) & 1
    place = jnp.stack([zlo, x]).astype(jnp.int32)
    blocks = me ^ jnp.array(ORDER, jnp.int32)
    head = head_weight.T
    bias = jnp.pad(
        lax.dynamic_slice(head_bias, (zlo * share,), (share,)),
        (0, padded - share),
        constant_values=-1.0,
    )[None, :]
    half, piece = tokens // 2, tokens // 2 // len(HIDDEN)

    live = {}

    def columns_of(chunks, low):
        first, size = starts[chunks[0]], sum(CHUNKS[c] for c in chunks)
        return jnp.where(
            low == 0, head[first : first + size], head[share + first : share + first + size]
        )

    for k, chunks in NEAR.items():
        live["given", k] = columns_of(chunks, 1 - zlo)
    for i, k in enumerate(HIDDEN):
        live["hidden", k] = lax.dynamic_slice(hidden, (x * half + i * piece, 0), (piece, width))
    live["table"] = jnp.concatenate(
        [
            (neg_owner * count + neg_index).astype(F32),
            teacher,
            query_len[:, None].astype(F32),
            passage_len[:, None].astype(F32),
        ],
        axis=1,
    )

    def near_of(j):
        for k, chunks in NEAR.items():
            if j in chunks:
                first = starts[j] - starts[chunks[0]]
                return live["near", k][first : first + CHUNKS[j]]

    def beside(j):
        return jnp.concatenate([columns_of((j,), zlo), near_of(j)], axis=1)

    def reps_of(groups):
        return jnp.concatenate([live["reps", g] for g in groups], axis=2)

    rows = lens = slopes = None
    rounds = max(COMPUTED) + 2
    for k in range(rounds + 1):
        sent = {}
        if 0 <= k - 1 < n:
            j = k - 1
            if ("two", j) not in live:
                live["two", j] = beside(j)
            sent["far", j] = swap(live["two", j], ZHI)
            sent["side", j] = swap(live["two", j], Y)
        if 0 <= k - 2 < n:
            sent["beyond", k - 2] = swap(live["far", k - 2], Y)
        for i in NEAR:
            if k == max(i - (i == 1), 0):
                sent["near", i] = swap(live["given", i], ZLO)
        if k in HIDDEN:
            sent["from_z", k] = swap(live["hidden", k], ZLO)
        if k - 1 in HIDDEN:
            sent["from_x", k - 1] = swap(live["from_z", k - 1], X)
        if k - 1 in TABLE:
            table, came = live["table"], live["table came"]
            both = [table, came]
            if TABLE[k - 1] == ZLO:
                both = [jnp.where(zlo == 0, table, came), jnp.where(zlo == 0, came, table)]
            live["table"] = jnp.concatenate(both)
        if k in TABLE:
            sent["table came"] = swap(live["table"], TABLE[k])
        if k == max(HIDDEN) + 2:
            by_z, by_x = ([live[name, i] for i in HIDDEN] for name in ("from_z", "from_x"))
            rows = arrange(blocks, x, hidden, by_z, by_x)
            pair_lens = live["table"][: 2 * count, 2 * neg_count :].astype(jnp.int32)
            lens = pair_lens.reshape(2, count, 2).transpose(0, 2, 1).reshape(-1)
        for g in range(len(GROUPS)):
            if k == PACKED[g]:
                arrays = [live[name, j] for j in GROUPS[g] for name in ("two", "far", "side", "beyond")]
                sent["quads", g] = pack([arrays[4 * i : 4 * i + 4] for i in range(len(GROUPS[g]))])
            if k == MOVED[g]:
                quads = sent if k == PACKED[g] else live
                sent["across", g] = swap(quads["quads", g], CORE)
            if k == COMPUTED[g]:
                first = starts[GROUPS[g][0]]
                quads, across = (
                    sent[key] if key in sent else live[key] for key in (("quads", g), ("across", g))
                )
                slopes, sent["reps", g] = forward(lens, rows, quads, across, bias, slopes, first)
        for groups, first in GATHERED:
            if first is None or not 0 <= k - first <= 3:
                continue
            if k == first:
                own = reps_of(groups)
            else:
                own = jnp.concatenate([live["gathered", groups], live["came", groups]], axis=1)
            live["gathered", groups] = own
            if k - first < 3:
                sent["came", groups] = swap(own, (ZHI, Y, CORE)[k - first])
        live.update(sent)
        if k > max(COMPUTED):
            continue
        held = list(sent)
        if k == 0:
            held.remove(("near", 1))
        if k == 1:
            held.append(("near", 1))
        if any(k in chunks[1:] for chunks in NEAR.values()):
            live["two", k] = beside(k)
            held.append(("two", k))
        held += [key for key in (("given", k + 1), ("hidden", k + 1)) if key in live]
        live.update(zip(held, lax.optimization_barrier([live[key] for key in held])))
    ids = live["table"][:, :neg_count].astype(jnp.int32)
    teachers = live["table"][:, neg_count : 2 * neg_count]
    owner = ids // count
    order = jnp.array(ORDER[::2], jnp.int32)
    group = jnp.sum(
        jnp.where(((owner ^ me) & ~4)[:, :, None] == order, jnp.arange(8, dtype=jnp.int32), 0),
        axis=2,
    )
    id_place = (group * 2 + ((owner >> 2) & 1)) * count + ids % count

    late = reps_of(GATHERED[-1][0])
    for bits in (ZHI, Y, CORE):
        late = jnp.concatenate([late, swap(late, bits)], axis=1)
    gathered = [live["gathered", groups] for groups, _ in GATHERED[:-1]] + [late]

    def scores(reps):
        return lax.dot_general(reps[0], reps[1], (((1,), (1,)), ((), ())), precision=HIGHEST)

    part = sum(scores(reps) for reps in gathered)
    margin_error, grads = margins(
        (part, swap(part, X), swap(part, ZLO), swap(part, ZLO | X)),
        id_place,
        teachers,
        slopes,
        gathered,
    )

    pairs, first = [], [None] * len(PIECES)

    def second(i):
        (keep_x, came_x), (keep_z, came_z) = first[i]
        mids = [
            (keep[1] + came[1].astype(F32)).astype(BF16)
            for keep, came in ((keep_x, came_x), (keep_z, came_z))
        ]
        nonlocal grads
        mid_x, mid_z, grads = lax.optimization_barrier((*mids, grads))
        pairs.append((keep_x[0] + came_x[0].astype(F32), swap(mid_x, ZLO)))
        pairs.append((keep_z[0] + came_z[0].astype(F32), swap(mid_z, X)))

    for i, (begin, steps) in enumerate(PIECES):
        heads = [live["quads" if begin < 8 else "across", g] for g in range(len(GROUPS))]
        outs = back_piece(place, grads, heads, begin, steps)
        send_x, keep_x, send_z, keep_z, grads = lax.optimization_barrier((*outs, grads))
        first[i] = ((keep_x, swap(send_x, X)), (keep_z, swap(send_z, ZLO)))
        if i >= 1:
            second(i - 1)
    second(len(PIECES) - 1)
    places = []
    for k in range(0, 16, 2):
        base = (me & ~4) ^ ORDER[k]
        places += [base, base | 4]
    hidden_grad = finish(jnp.stack(places).astype(jnp.int32), pairs)
    return (lax.dynamic_slice(margin_error, (zlo * count, 0), (count, neg_count)), hidden_grad)


def solution(mesh):
    square = mesh.shape["dp"] == 16 and mesh.shape["vocab"] == 2
    return jax.shard_map(
        by_squares if square else any_mesh,
        mesh=mesh,
        in_specs=(
            P("dp", None),
            P("dp", "vocab"),
            P("vocab"),
            P("dp"),
            P("dp"),
            P("dp", None),
            P("dp", None),
            P("dp", None),
        ),
        out_specs=(P("dp", None), P(("dp", "vocab"), None)),
        check_vma=False,
    )
```

```python
import jax
import jax.numpy as jnp
from jax import lax
from jax.experimental import pallas as pl
from jax.experimental.pallas import tpu as pltpu
from jax.sharding import PartitionSpec as P

LQ = 32
LP = 64


TAU = 0.05
AXES = ("dp", "vocab")
F32 = jnp.float32
BF16 = jnp.bfloat16
X, CORE, Y, ZLO, ZHI = 1, 2, 4, 8, 16
ORDER = (0, 4, 8, 12, 2, 6, 10, 14, 1, 5, 9, 13, 3, 7, 11, 15)
CHUNKS = (256,) + (512,) * 7 + (160,)
NEAR = {0: (0,), 1: (1, 2), 3: (3, 4), 5: (5, 6), 7: (7, 8)}
HIDDEN = (2, 4)
TABLE = {1: ZLO, 2: ZHI, 10: Y, 11: CORE}
GROUPS = ((0,), (1, 2), (3,), (4,), (5,), (6,), (7,), (8,))
PACKED = (3, 5, 6, 7, 8, 9, 10, 11)
MOVED = (4, 6, 7, 8, 8, 9, 10, 11)
COMPUTED = (6, 7, 7, 8, 8, 9, 10, 11)
GATHERED = (((0, 1, 2), 9), ((3, 4, 5), 10), ((6, 7), None))
PIECES = ((0, 8), (8, 4), (12, 4))
HIGHEST = lax.Precision.HIGHEST
NO_COST = pl.CostEstimate(flops=0, bytes_accessed=0, transcendentals=0)


def soft_pool(token_logits, token_mask):
    activation = jnp.log1p(jnp.maximum(token_logits, 0.0))
    weights = jnp.exp(activation / TAU) * token_mask[:, :, None]
    summed = jnp.sum(weights, axis=1)
    valid_count = jnp.sum(token_mask, axis=1)[:, None]
    return (TAU * jnp.log(summed / valid_count), weights / summed[:, None, :])


def lengths_mask(lengths, span):
    return (jnp.arange(span)[None, :] < lengths[:, None]).astype(jnp.float32)


def any_mesh(
    hidden, head_weight, head_bias, query_len, passage_len, neg_owner, neg_index, teacher
):
    query_count = neg_owner.shape[0]
    neg_count = neg_owner.shape[1]
    owners = lax.axis_size("dp")
    head_full = lax.all_gather(head_weight, "dp", axis=0, tiled=True)
    vocab_width = head_full.shape[1]
    logits = jnp.dot(hidden, head_full, preferred_element_type=jnp.float32) + head_bias[None, :]
    query_tokens = query_count * LQ
    query_rep, query_weights = soft_pool(
        logits[:query_tokens].reshape(query_count, LQ, vocab_width), lengths_mask(query_len, LQ)
    )
    passage_rep, passage_weights = soft_pool(
        logits[query_tokens:].reshape(query_count, LP, vocab_width), lengths_mask(passage_len, LP)
    )
    gathered = lax.all_gather(passage_rep, "dp", axis=0, tiled=True)
    passage_ids = neg_owner * query_count + neg_index
    neg_rows = jnp.take(gathered, passage_ids.reshape(-1), axis=0).reshape(
        query_count, neg_count, vocab_width
    )
    pos_part = jnp.sum(query_rep * passage_rep, axis=1)
    neg_part = jnp.sum(query_rep[:, None, :] * neg_rows, axis=2)
    positive, negative = lax.psum((pos_part, neg_part), "vocab")
    margin_error = positive[:, None] - negative - teacher
    grad_pos = jnp.sum(margin_error, axis=1)
    grad_neg = -margin_error
    query_grad = grad_pos[:, None] * passage_rep + jnp.sum(grad_neg[:, :, None] * neg_rows, axis=1)
    neg_terms = (grad_neg[:, :, None] * query_rep[:, None, :]).reshape(-1, vocab_width)
    scattered = jax.ops.segment_sum(
        neg_terms, passage_ids.reshape(-1), num_segments=owners * query_count
    )
    returned_grad = lax.psum_scatter(scattered, "dp", scatter_dimension=0, tiled=True)
    passage_grad = grad_pos[:, None] * query_rep + returned_grad
    relu_slope = (logits > 0).astype(jnp.float32) / (1.0 + jnp.maximum(logits, 0.0))
    d_query = (query_grad[:, None, :] * query_weights).reshape(-1, vocab_width)
    d_passage = (passage_grad[:, None, :] * passage_weights).reshape(-1, vocab_width)
    logit_grad = (jnp.concatenate([d_query, d_passage], axis=0) * relu_slope).astype(jnp.bfloat16)
    hidden_grad = lax.psum_scatter(
        lax.dot_general(
            logit_grad, head_full, (((1,), (1,)), ((), ())), preferred_element_type=jnp.float32
        ),
        "vocab",
        scatter_dimension=0,
        tiled=True,
    )
    return (margin_error, hidden_grad)


def in_hbm(*arrays):
    return [pltpu.with_memory_space_constraint(a, pltpu.HBM) for a in arrays]


def in_vmem(array):
    return pltpu.with_memory_space_constraint(array, pltpu.VMEM)


def swap(array, bits):
    return lax.ppermute(array, AXES, [(i, i ^ bits) for i in range(32)])


def arrange(places, x, hidden, by_z, by_x):
    rows, width = hidden.shape
    block = width // 16
    pieces = [*by_z, *by_x]
    step = pieces[0].shape[0]
    n = rows // step

    def kernel(places, hidden, *refs):
        sources, out = refs[:-1], refs[-1]

        def put(source):
            for k in range(16):
                lanes = pl.ds(pl.multiple_of(places[k] * block, block), block)
                out[:, k * block : (k + 1) * block] = source[:, lanes]

        at = pl.program_id(0)

        @pl.when(at < n)
        def _():
            put(hidden)

        for i, source in enumerate(sources):

            @pl.when(at == n + i)
            def _():
                put(source)

    def there(i, places):
        own = places[0] // 4 % 2
        piece = jnp.maximum(i - n, 0)
        half = (piece // len(by_z) + places[16]) % 2
        other = (1 - own) * n + half * len(by_z) + piece % len(by_z)
        return jnp.where(i < n, own * n + i, other), 0

    return pl.pallas_call(
        kernel,
        grid_spec=pltpu.PrefetchScalarGridSpec(
            num_scalar_prefetch=1,
            grid=(2 * n,),
            in_specs=[pl.BlockSpec((step, width), lambda i, places: (jnp.minimum(i, n - 1), 0))]
            + [pl.BlockSpec((step, width), lambda i, places: (0, 0))] * len(pieces),
            out_specs=pl.BlockSpec((step, width), there),
        ),
        out_shape=pltpu.VMEM((2 * rows, width), hidden.dtype),
        compiler_params=pltpu.CompilerParams(vmem_limit_bytes=24 * 2**20),
        cost_estimate=NO_COST,
        name="arrange",
    )(jnp.concatenate([places, x[None]]).astype(jnp.int32), hidden, *pieces)


def pack(groups):
    n = len(groups)
    block = groups[0][0].shape[1] // 2
    heights = [group[0].shape[0] for group in groups]
    step = 256 if all(h % 256 == 0 for h in heights) else heights[0]
    ends = [sum(heights[: i + 1]) // step for i in range(n)]
    firsts = [0] + ends[:-1]

    def kernel(*refs):
        out = refs[-1]
        for i in range(n):

            @pl.when((pl.program_id(0) >= firsts[i]) & (pl.program_id(0) < ends[i]))
            def _():
                for k in range(8):
                    out[k] = refs[4 * i + k // 2][:, k % 2 * block : (k % 2 + 1) * block]

    specs = []
    for i in range(n):
        last = heights[i] // step - 1
        specs += [
            pl.BlockSpec(
                (step, 2 * block), lambda r, i=i, last=last: (jnp.clip(r - firsts[i], 0, last), 0)
            )
        ] * 4
    return pl.pallas_call(
        kernel,
        grid=(ends[-1],),
        in_specs=specs,
        out_specs=pl.BlockSpec((8, step, block), lambda r: (0, r, 0)),
        out_shape=pltpu.HBM((8, sum(heights), block), BF16),
        compiler_params=pltpu.CompilerParams(vmem_limit_bytes=24 * 2**20),
        cost_estimate=NO_COST,
        name="pack",
    )(*in_hbm(*[a for group in groups for a in group]))


def forward(lens, rows, near, across, bias, slopes, start):
    tokens, depth = rows.shape
    blocks, wide, block = near.shape
    tile = 256
    tiles = -(-wide // tile)
    count = lens.shape[0] // 4
    spans = [LQ] * count + [LP] * count

    def kernel(lens, rows, near, across, bias, *refs):
        slope, reps = refs[-2:]
        by_rows = (((1,), (1,)), ((), ()))
        logits = bias[...]
        for k in range(2 * blocks):
            head = (near if k < blocks else across)[k % blocks]
            logits = logits + lax.dot_general(
                rows[:, k * block : (k + 1) * block], head, by_rows, preferred_element_type=F32
            )
        if wide % tile:
            lanes = pl.program_id(0) * tile + lax.broadcasted_iota(jnp.int32, logits.shape, 1)
            logits = jnp.where(lanes < wide, logits, -1.0)
        at = 0
        for b in range(2):
            for i, span in enumerate(spans):
                x = logits[at : at + span]
                length = lens[b * 2 * count + i]
                grown = 1.0 + jnp.maximum(x, 0.0)
                p2 = grown * grown
                p4 = p2 * p2
                p8 = p4 * p4
                valid = lax.broadcasted_iota(jnp.int32, (span, tile), 0) < length
                p19 = jnp.where(valid, p8 * p8 * (p2 * grown), 0.0)
                summed = jnp.sum(p19 * grown, axis=0, keepdims=True)
                rep = TAU * jnp.log(summed / length.astype(F32))
                reps[i // count, pl.ds(b * count + i % count, 1), :] = rep
                slope[0, at : at + span, :] = jnp.where(x > 0, p19, 0.0) * (1.0 / summed)
                at += span

    first = start // tile
    old = [] if slopes is None else [slopes]
    return pl.pallas_call(
        kernel,
        grid_spec=pltpu.PrefetchScalarGridSpec(
            num_scalar_prefetch=1,
            grid=(tiles,),
            in_specs=[
                pl.BlockSpec(memory_space=pltpu.VMEM),
                pl.BlockSpec((blocks, tile, block), lambda c, lens: (0, c, 0)),
                pl.BlockSpec((blocks, tile, block), lambda c, lens: (0, c, 0)),
                pl.BlockSpec((1, tile), lambda c, lens: (0, first + c)),
            ]
            + [pl.BlockSpec(memory_space=pl.ANY)] * len(old),
            out_specs=[
                pl.BlockSpec((1, tokens, tile), lambda c, lens: (first + c, 0, 0)),
                pl.BlockSpec((2, 2 * count, tile), lambda c, lens: (0, 0, c)),
            ],
        ),
        out_shape=[
            pltpu.HBM((bias.shape[1] // tile, tokens, tile), F32),
            jax.ShapeDtypeStruct((2, 2 * count, tiles * tile), F32),
        ],
        input_output_aliases={5: 0} if old else {},
        compiler_params=pltpu.CompilerParams(vmem_limit_bytes=24 * 2**20),
        cost_estimate=NO_COST,
        name=f"forward{start}",
    )(lens, in_vmem(rows), *in_hbm(near), across, bias, *in_hbm(*old))


def margins(parts, id_place, teachers, slopes, gathered):
    tiles, tokens, tile = slopes.shape
    queries, neg_count = teachers.shape
    pair = queries // 8
    n = len(gathered)
    ends = [sum(reps.shape[2] for reps in gathered[: i + 1]) // tile for i in range(n)]
    firsts = [0] + ends[:-1]
    batch = 4

    def kernel(s0, s1, s2, s3, ids, teach, slope, *refs):
        gathered, (margin, grad, coeff, coeff_t) = refs[:n], refs[n:]
        step = pl.program_id(0)

        @pl.when(step == 0)
        def _():
            score = (s0[...] + s1[...]) + (s2[...] + s3[...])
            lanes = lax.broadcasted_iota(jnp.int32, score.shape, 1)
            eye = lax.broadcasted_iota(jnp.int32, score.shape, 0) == lanes
            positive = jnp.sum(jnp.where(eye, score, 0.0), axis=1, keepdims=True)
            total = jnp.zeros_like(score)
            grad_pos = jnp.zeros_like(positive)
            for k in range(neg_count):
                chosen = ids[:, k : k + 1] == lanes
                negative = jnp.sum(jnp.where(chosen, score, 0.0), axis=1, keepdims=True)
                error = positive - negative - teach[:, k : k + 1]
                margin[:, k : k + 1] = error
                total = total - jnp.where(chosen, error, 0.0)
                grad_pos = grad_pos + error
            total = total + jnp.where(eye, grad_pos, 0.0)
            coeff[...] = total
            coeff_t[...] = total.T

        def fill(t, reps, first):
            there = pl.ds(pl.multiple_of((step * batch + t - first) * tile, tile), tile)
            here = pl.ds(pl.multiple_of((step * batch + t) * tile, tile), tile)
            grad_q = jnp.dot(
                coeff[:pair], reps[1, :, there], precision=HIGHEST, preferred_element_type=F32
            )
            grad_p = jnp.dot(
                coeff_t[:pair], reps[0, :, there], precision=HIGHEST, preferred_element_type=F32
            )
            at = 0
            for b in range(2):
                for span, part in ((LQ, grad_q), (LP, grad_p)):
                    for i in range(pair // 2):
                        row = b * (pair // 2) + i
                        grad[at : at + span, here] = (
                            slope[t, at : at + span, :] * part[row : row + 1]
                        ).astype(BF16)
                        at += span

        for t in range(batch):
            for reps, first, end in zip(gathered, firsts, ends):

                @pl.when((step * batch + t >= first) & (step * batch + t < end))
                def _():
                    fill(t, reps, first)

    square = pl.BlockSpec((queries, queries), lambda c: (0, 0))
    listed = pl.BlockSpec((queries, neg_count), lambda c: (0, 0))
    return pl.pallas_call(
        kernel,
        grid=(tiles // batch,),
        in_specs=[square] * 4
        + [listed] * 2
        + [pl.BlockSpec((batch, tokens, tile), lambda c: (c, 0, 0))]
        + [pl.BlockSpec(memory_space=pltpu.VMEM)] * n,
        out_specs=[listed, pl.BlockSpec(memory_space=pltpu.VMEM)],
        out_shape=[
            jax.ShapeDtypeStruct((queries, neg_count), F32),
            pltpu.VMEM((tokens, tiles * tile), BF16),
        ],
        scratch_shapes=[pltpu.VMEM((queries, queries), F32)] * 2,
        compiler_params=pltpu.CompilerParams(vmem_limit_bytes=24 * 2**20),
        name="margins",
    )(*parts, id_place, teachers, *in_hbm(slopes), *gathered)


def back_piece(place, grads, heads, begin, steps):
    n = len(heads)
    rows, block = grads.shape[0], heads[0].shape[2]
    half = rows // 4

    def kernel(place, grad, *refs):
        heads, (send_x, keep_x, send_z, keep_z, total) = refs[:n], refs[n:]
        sums, start = None, 0
        for head in heads:
            wide = head.shape[1]
            part = jnp.dot(grad[:, start : start + wide], head[0], preferred_element_type=F32)
            sums = part if sums is None else sums + part
            start += wide
        total[...] = sums
        zlo, x = place[0], place[1]

        def rows_of(z, x):
            return total[pl.ds((2 * z + x) * half, half), :]

        @pl.when(pl.program_id(0) < steps // 2)
        def _():
            keep_x[0], keep_x[1] = rows_of(zlo, x), rows_of(1 - zlo, x)
            send_x[0] = rows_of(zlo, 1 - x).astype(BF16)
            send_x[1] = rows_of(1 - zlo, 1 - x).astype(BF16)

        @pl.when(pl.program_id(0) >= steps // 2)
        def _():
            keep_z[0], keep_z[1] = rows_of(zlo, x), rows_of(zlo, 1 - x)
            send_z[0] = rows_of(1 - zlo, x).astype(BF16)
            send_z[1] = rows_of(1 - zlo, 1 - x).astype(BF16)

    some = [
        pl.BlockSpec((1, h.shape[1], block), lambda d, place: (begin % 8 + d, 0, 0))
        for h in heads
    ]
    last = steps // 2 - 1
    by_x = pl.BlockSpec(
        (2, half, block), lambda d, place: (0, 0, jnp.minimum(d, last) ^ place[0])
    )
    by_z = pl.BlockSpec(
        (2, half, block), lambda d, place: (0, 0, jnp.maximum(d - last - 1, 0) ^ place[0])
    )
    shape = (2, half, steps // 2 * block)
    return pl.pallas_call(
        kernel,
        grid_spec=pltpu.PrefetchScalarGridSpec(
            num_scalar_prefetch=1,
            grid=(steps,),
            in_specs=[pl.BlockSpec(memory_space=pltpu.VMEM)] + some,
            out_specs=[by_x, by_x, by_z, by_z],
            scratch_shapes=[pltpu.VMEM((rows, block), F32)],
        ),
        out_shape=[pltpu.HBM(shape, t) for t in (BF16, F32, BF16, F32)],
        compiler_params=pltpu.CompilerParams(vmem_limit_bytes=24 * 2**20),
        cost_estimate=pl.CostEstimate(
            flops=2 * rows * grads.shape[1] * steps * block,
            bytes_accessed=2 * grads.shape[1] * steps * block + 3 * rows * steps * block,
            transcendentals=0,
        ),
        name=f"back{begin}",
    )(place, in_vmem(grads), *in_hbm(*heads))


def finish(places, pairs):
    rows = pairs[0][0].shape[0]
    widths = [pair[0].shape[1] for pair in pairs]
    block = sum(widths) // 16
    step = rows // 2

    def kernel(places, *refs):
        out = refs[-1]
        at = 0
        for i, width in enumerate(widths):
            for k in range(width // block):
                cols = slice(k * block, (k + 1) * block)
                lanes = pl.ds(pl.multiple_of(places[at + k] * block, block), block)
                out[:, lanes] = refs[2 * i][:, cols] + refs[2 * i + 1][:, cols].astype(F32)
            at += width // block

    return pl.pallas_call(
        kernel,
        grid_spec=pltpu.PrefetchScalarGridSpec(
            num_scalar_prefetch=1,
            grid=(rows // step,),
            in_specs=[
                pl.BlockSpec((step, width), lambda r, places: (r, 0)) for width in widths for _ in range(2)
            ],
            out_specs=pl.BlockSpec((step, 16 * block), lambda r, places: (r, 0)),
        ),
        out_shape=jax.ShapeDtypeStruct((rows, 16 * block), F32),
        compiler_params=pltpu.CompilerParams(vmem_limit_bytes=24 * 2**20),
        name="finish",
    )(places, *[a for pair in pairs for a in pair])


def by_squares(
    hidden, head_weight, head_bias, query_len, passage_len, neg_owner, neg_index, teacher
):
    count, neg_count = neg_owner.shape
    tokens, width = hidden.shape
    depth, columns = head_weight.shape
    share = columns // 2
    padded = -(-share // 256) * 256
    n = len(CHUNKS)
    starts = [sum(CHUNKS[:j]) for j in range(n)]
    me = lax.axis_index("dp")
    x = lax.axis_index("vocab")
    zlo = (me >> 2) & 1
    place = jnp.stack([zlo, x]).astype(jnp.int32)
    blocks = me ^ jnp.array(ORDER, jnp.int32)
    head = head_weight.T
    bias = jnp.pad(
        lax.dynamic_slice(head_bias, (zlo * share,), (share,)),
        (0, padded - share),
        constant_values=-1.0,
    )[None, :]
    half, piece = tokens // 2, tokens // 2 // len(HIDDEN)

    live = {}

    def columns_of(chunks, low):
        first, size = starts[chunks[0]], sum(CHUNKS[c] for c in chunks)
        return jnp.where(
            low == 0, head[first : first + size], head[share + first : share + first + size]
        )

    for k, chunks in NEAR.items():
        live["given", k] = columns_of(chunks, 1 - zlo)
    for i, k in enumerate(HIDDEN):
        live["hidden", k] = lax.dynamic_slice(hidden, (x * half + i * piece, 0), (piece, width))
    live["table"] = jnp.concatenate(
        [
            (neg_owner * count + neg_index).astype(F32),
            teacher,
            query_len[:, None].astype(F32),
            passage_len[:, None].astype(F32),
        ],
        axis=1,
    )

    def near_of(j):
        for k, chunks in NEAR.items():
            if j in chunks:
                first = starts[j] - starts[chunks[0]]
                return live["near", k][first : first + CHUNKS[j]]

    def beside(j):
        return jnp.concatenate([columns_of((j,), zlo), near_of(j)], axis=1)

    def reps_of(groups):
        return jnp.concatenate([live["reps", g] for g in groups], axis=2)

    rows = lens = slopes = None
    rounds = max(COMPUTED) + 2
    for k in range(rounds + 1):
        sent = {}
        if 0 <= k - 1 < n:
            j = k - 1
            if ("two", j) not in live:
                live["two", j] = beside(j)
            sent["far", j] = swap(live["two", j], ZHI)
            sent["side", j] = swap(live["two", j], Y)
        if 0 <= k - 2 < n:
            sent["beyond", k - 2] = swap(live["far", k - 2], Y)
        for i in NEAR:
            if k == max(i - (i == 1), 0):
                sent["near", i] = swap(live["given", i], ZLO)
        if k in HIDDEN:
            sent["from_z", k] = swap(live["hidden", k], ZLO)
        if k - 1 in HIDDEN:
            sent["from_x", k - 1] = swap(live["from_z", k - 1], X)
        if k - 1 in TABLE:
            table, came = live["table"], live["table came"]
            both = [table, came]
            if TABLE[k - 1] == ZLO:
                both = [jnp.where(zlo == 0, table, came), jnp.where(zlo == 0, came, table)]
            live["table"] = jnp.concatenate(both)
        if k in TABLE:
            sent["table came"] = swap(live["table"], TABLE[k])
        if k == max(HIDDEN) + 2:
            by_z, by_x = ([live[name, i] for i in HIDDEN] for name in ("from_z", "from_x"))
            rows = arrange(blocks, x, hidden, by_z, by_x)
            pair_lens = live["table"][: 2 * count, 2 * neg_count :].astype(jnp.int32)
            lens = pair_lens.reshape(2, count, 2).transpose(0, 2, 1).reshape(-1)
        for g in range(len(GROUPS)):
            if k == PACKED[g]:
                arrays = [live[name, j] for j in GROUPS[g] for name in ("two", "far", "side", "beyond")]
                sent["quads", g] = pack([arrays[4 * i : 4 * i + 4] for i in range(len(GROUPS[g]))])
            if k == MOVED[g]:
                quads = sent if k == PACKED[g] else live
                sent["across", g] = swap(quads["quads", g], CORE)
            if k == COMPUTED[g]:
                first = starts[GROUPS[g][0]]
                quads, across = (
                    sent[key] if key in sent else live[key] for key in (("quads", g), ("across", g))
                )
                slopes, sent["reps", g] = forward(lens, rows, quads, across, bias, slopes, first)
        for groups, first in GATHERED:
            if first is None or not 0 <= k - first <= 3:
                continue
            if k == first:
                own = reps_of(groups)
            else:
                own = jnp.concatenate([live["gathered", groups], live["came", groups]], axis=1)
            live["gathered", groups] = own
            if k - first < 3:
                sent["came", groups] = swap(own, (ZHI, Y, CORE)[k - first])
        live.update(sent)
        if k > max(COMPUTED):
            continue
        held = list(sent)
        if k == 0:
            held.remove(("near", 1))
        if k == 1:
            held.append(("near", 1))
        if any(k in chunks[1:] for chunks in NEAR.values()):
            live["two", k] = beside(k)
            held.append(("two", k))
        held += [key for key in (("given", k + 1), ("hidden", k + 1)) if key in live]
        live.update(zip(held, lax.optimization_barrier([live[key] for key in held])))
    ids = live["table"][:, :neg_count].astype(jnp.int32)
    teachers = live["table"][:, neg_count : 2 * neg_count]
    owner = ids // count
    order = jnp.array(ORDER[::2], jnp.int32)
    group = jnp.sum(
        jnp.where(((owner ^ me) & ~4)[:, :, None] == order, jnp.arange(8, dtype=jnp.int32), 0),
        axis=2,
    )
    id_place = (group * 2 + ((owner >> 2) & 1)) * count + ids % count

    late = reps_of(GATHERED[-1][0])
    late = jnp.concatenate([late] + [swap(late, bits) for bits in (ZHI, Y, ZHI | Y)], axis=1)
    late = jnp.concatenate([late, swap(late, CORE)], axis=1)
    gathered = [live["gathered", groups] for groups, _ in GATHERED[:-1]] + [late]

    def scores(reps):
        return lax.dot_general(reps[0], reps[1], (((1,), (1,)), ((), ())), precision=HIGHEST)

    part = sum(scores(reps) for reps in gathered)
    margin_error, grads = margins(
        (part, swap(part, X), swap(part, ZLO), swap(part, ZLO | X)),
        id_place,
        teachers,
        slopes,
        gathered,
    )

    pairs, first = [], [None] * len(PIECES)

    def second(i):
        (keep_x, came_x), (keep_z, came_z) = first[i]
        mids = [
            (keep[1] + came[1].astype(F32)).astype(BF16)
            for keep, came in ((keep_x, came_x), (keep_z, came_z))
        ]
        nonlocal grads
        mid_x, mid_z, grads = lax.optimization_barrier((*mids, grads))
        pairs.append((keep_x[0] + came_x[0].astype(F32), swap(mid_x, ZLO)))
        pairs.append((keep_z[0] + came_z[0].astype(F32), swap(mid_z, X)))

    for i, (begin, steps) in enumerate(PIECES):
        heads = [live["quads" if begin < 8 else "across", g] for g in range(len(GROUPS))]
        outs = back_piece(place, grads, heads, begin, steps)
        send_x, keep_x, send_z, keep_z, grads = lax.optimization_barrier((*outs, grads))
        first[i] = ((keep_x, swap(send_x, X)), (keep_z, swap(send_z, ZLO)))
        if i >= 1:
            second(i - 1)
    second(len(PIECES) - 1)
    places = []
    for k in range(0, 16, 2):
        base = (me & ~4) ^ ORDER[k]
        places += [base, base | 4]
    hidden_grad = finish(jnp.stack(places).astype(jnp.int32), pairs)
    return (lax.dynamic_slice(margin_error, (zlo * count, 0), (count, neg_count)), hidden_grad)


def solution(mesh):
    square = mesh.shape["dp"] == 16 and mesh.shape["vocab"] == 2
    return jax.shard_map(
        by_squares if square else any_mesh,
        mesh=mesh,
        in_specs=(
            P("dp", None),
            P("dp", "vocab"),
            P("vocab"),
            P("dp"),
            P("dp"),
            P("dp", None),
            P("dp", None),
            P("dp", None),
        ),
        out_specs=(P("dp", None), P(("dp", "vocab"), None)),
        check_vma=False,
    )
```

```python
import jax
import jax.numpy as jnp
from jax import lax
from jax.experimental import pallas as pl
from jax.experimental.pallas import tpu as pltpu
from jax.sharding import PartitionSpec as P

LQ = 32
LP = 64


TAU = 0.05
AXES = ("dp", "vocab")
F32 = jnp.float32
BF16 = jnp.bfloat16
X, CORE, Y, ZLO, ZHI = 1, 2, 4, 8, 16
ORDER = (0, 4, 8, 12, 2, 6, 10, 14, 1, 5, 9, 13, 3, 7, 11, 15)
CHUNKS = (256,) + (512,) * 7 + (160,)
NEAR = {0: (0,), 1: (1, 2), 3: (3, 4), 5: (5, 6), 7: (7, 8)}
HIDDEN = (2, 4)
TABLE = {1: ZLO, 2: ZHI, 10: Y, 11: CORE}
GROUPS = ((0,), (1, 2), (3,), (4,), (5,), (6,), (7,), (8,))
PACKED = (3, 5, 6, 7, 8, 9, 10, 11)
MOVED = (4, 6, 7, 8, 8, 9, 10, 11)
COMPUTED = (6, 7, 7, 8, 8, 9, 10, 11)
GATHERED = (((0, 1, 2), 9), ((3, 4, 5), 10), ((6, 7), None))
PIECES = ((0, 8), (8, 4), (12, 4))
HIGHEST = lax.Precision.HIGHEST
NO_COST = pl.CostEstimate(flops=0, bytes_accessed=0, transcendentals=0)


def soft_pool(token_logits, token_mask):
    activation = jnp.log1p(jnp.maximum(token_logits, 0.0))
    weights = jnp.exp(activation / TAU) * token_mask[:, :, None]
    summed = jnp.sum(weights, axis=1)
    valid_count = jnp.sum(token_mask, axis=1)[:, None]
    return (TAU * jnp.log(summed / valid_count), weights / summed[:, None, :])


def lengths_mask(lengths, span):
    return (jnp.arange(span)[None, :] < lengths[:, None]).astype(jnp.float32)


def any_mesh(
    hidden, head_weight, head_bias, query_len, passage_len, neg_owner, neg_index, teacher
):
    query_count = neg_owner.shape[0]
    neg_count = neg_owner.shape[1]
    owners = lax.axis_size("dp")
    head_full = lax.all_gather(head_weight, "dp", axis=0, tiled=True)
    vocab_width = head_full.shape[1]
    logits = jnp.dot(hidden, head_full, preferred_element_type=jnp.float32) + head_bias[None, :]
    query_tokens = query_count * LQ
    query_rep, query_weights = soft_pool(
        logits[:query_tokens].reshape(query_count, LQ, vocab_width), lengths_mask(query_len, LQ)
    )
    passage_rep, passage_weights = soft_pool(
        logits[query_tokens:].reshape(query_count, LP, vocab_width), lengths_mask(passage_len, LP)
    )
    gathered = lax.all_gather(passage_rep, "dp", axis=0, tiled=True)
    passage_ids = neg_owner * query_count + neg_index
    neg_rows = jnp.take(gathered, passage_ids.reshape(-1), axis=0).reshape(
        query_count, neg_count, vocab_width
    )
    pos_part = jnp.sum(query_rep * passage_rep, axis=1)
    neg_part = jnp.sum(query_rep[:, None, :] * neg_rows, axis=2)
    positive, negative = lax.psum((pos_part, neg_part), "vocab")
    margin_error = positive[:, None] - negative - teacher
    grad_pos = jnp.sum(margin_error, axis=1)
    grad_neg = -margin_error
    query_grad = grad_pos[:, None] * passage_rep + jnp.sum(grad_neg[:, :, None] * neg_rows, axis=1)
    neg_terms = (grad_neg[:, :, None] * query_rep[:, None, :]).reshape(-1, vocab_width)
    scattered = jax.ops.segment_sum(
        neg_terms, passage_ids.reshape(-1), num_segments=owners * query_count
    )
    returned_grad = lax.psum_scatter(scattered, "dp", scatter_dimension=0, tiled=True)
    passage_grad = grad_pos[:, None] * query_rep + returned_grad
    relu_slope = (logits > 0).astype(jnp.float32) / (1.0 + jnp.maximum(logits, 0.0))
    d_query = (query_grad[:, None, :] * query_weights).reshape(-1, vocab_width)
    d_passage = (passage_grad[:, None, :] * passage_weights).reshape(-1, vocab_width)
    logit_grad = (jnp.concatenate([d_query, d_passage], axis=0) * relu_slope).astype(jnp.bfloat16)
    hidden_grad = lax.psum_scatter(
        lax.dot_general(
            logit_grad, head_full, (((1,), (1,)), ((), ())), preferred_element_type=jnp.float32
        ),
        "vocab",
        scatter_dimension=0,
        tiled=True,
    )
    return (margin_error, hidden_grad)


def in_hbm(*arrays):
    return [pltpu.with_memory_space_constraint(a, pltpu.HBM) for a in arrays]


def in_vmem(array):
    return pltpu.with_memory_space_constraint(array, pltpu.VMEM)


def swap(array, bits):
    return lax.ppermute(array, AXES, [(i, i ^ bits) for i in range(32)])


def arrange(places, x, hidden, by_z, by_x):
    rows, width = hidden.shape
    block = width // 16
    pieces = [*by_z, *by_x]
    step = pieces[0].shape[0]
    n = rows // step

    def kernel(places, hidden, *refs):
        sources, out = refs[:-1], refs[-1]

        def put(source):
            for k in range(16):
                lanes = pl.ds(pl.multiple_of(places[k] * block, block), block)
                out[:, k * block : (k + 1) * block] = source[:, lanes]

        at = pl.program_id(0)

        @pl.when(at < n)
        def _():
            put(hidden)

        for i, source in enumerate(sources):

            @pl.when(at == n + i)
            def _():
                put(source)

    def there(i, places):
        own = places[0] // 4 % 2
        piece = jnp.maximum(i - n, 0)
        half = (piece // len(by_z) + places[16]) % 2
        other = (1 - own) * n + half * len(by_z) + piece % len(by_z)
        return jnp.where(i < n, own * n + i, other), 0

    return pl.pallas_call(
        kernel,
        grid_spec=pltpu.PrefetchScalarGridSpec(
            num_scalar_prefetch=1,
            grid=(2 * n,),
            in_specs=[pl.BlockSpec((step, width), lambda i, places: (jnp.minimum(i, n - 1), 0))]
            + [pl.BlockSpec((step, width), lambda i, places: (0, 0))] * len(pieces),
            out_specs=pl.BlockSpec((step, width), there),
        ),
        out_shape=pltpu.VMEM((2 * rows, width), hidden.dtype),
        compiler_params=pltpu.CompilerParams(vmem_limit_bytes=24 * 2**20),
        cost_estimate=NO_COST,
        name="arrange",
    )(jnp.concatenate([places, x[None]]).astype(jnp.int32), hidden, *pieces)


def pack(groups):
    n = len(groups)
    block = groups[0][0].shape[1] // 2
    heights = [group[0].shape[0] for group in groups]
    step = 256 if all(h % 256 == 0 for h in heights) else heights[0]
    ends = [sum(heights[: i + 1]) // step for i in range(n)]
    firsts = [0] + ends[:-1]

    def kernel(*refs):
        out = refs[-1]
        for i in range(n):

            @pl.when((pl.program_id(0) >= firsts[i]) & (pl.program_id(0) < ends[i]))
            def _():
                for k in range(8):
                    out[k] = refs[4 * i + k // 2][:, k % 2 * block : (k % 2 + 1) * block]

    specs = []
    for i in range(n):
        last = heights[i] // step - 1
        specs += [
            pl.BlockSpec(
                (step, 2 * block), lambda r, i=i, last=last: (jnp.clip(r - firsts[i], 0, last), 0)
            )
        ] * 4
    return pl.pallas_call(
        kernel,
        grid=(ends[-1],),
        in_specs=specs,
        out_specs=pl.BlockSpec((8, step, block), lambda r: (0, r, 0)),
        out_shape=pltpu.HBM((8, sum(heights), block), BF16),
        compiler_params=pltpu.CompilerParams(vmem_limit_bytes=24 * 2**20),
        cost_estimate=NO_COST,
        name="pack",
    )(*in_hbm(*[a for group in groups for a in group]))


def forward(lens, rows, near, across, bias, slopes, start):
    tokens, depth = rows.shape
    blocks, wide, block = near.shape
    tile = 256
    tiles = -(-wide // tile)
    count = lens.shape[0] // 4
    spans = [LQ] * count + [LP] * count

    def kernel(lens, rows, near, across, bias, *refs):
        slope, reps = refs[-2:]
        by_rows = (((1,), (1,)), ((), ()))
        logits = bias[...]
        for k in range(2 * blocks):
            head = (near if k < blocks else across)[k % blocks]
            logits = logits + lax.dot_general(
                rows[:, k * block : (k + 1) * block], head, by_rows, preferred_element_type=F32
            )
        if wide % tile:
            lanes = pl.program_id(0) * tile + lax.broadcasted_iota(jnp.int32, logits.shape, 1)
            logits = jnp.where(lanes < wide, logits, -1.0)
        at = 0
        for b in range(2):
            for i, span in enumerate(spans):
                x = logits[at : at + span]
                length = lens[b * 2 * count + i]
                grown = 1.0 + jnp.maximum(x, 0.0)
                p2 = grown * grown
                p4 = p2 * p2
                p8 = p4 * p4
                valid = lax.broadcasted_iota(jnp.int32, (span, tile), 0) < length
                p19 = jnp.where(valid, p8 * p8 * (p2 * grown), 0.0)
                summed = jnp.sum(p19 * grown, axis=0, keepdims=True)
                rep = TAU * jnp.log(summed / length.astype(F32))
                reps[i // count, pl.ds(b * count + i % count, 1), :] = rep
                slope[0, at : at + span, :] = jnp.where(x > 0, p19, 0.0) * (1.0 / summed)
                at += span

    first = start // tile
    old = [] if slopes is None else [slopes]
    return pl.pallas_call(
        kernel,
        grid_spec=pltpu.PrefetchScalarGridSpec(
            num_scalar_prefetch=1,
            grid=(tiles,),
            in_specs=[
                pl.BlockSpec(memory_space=pltpu.VMEM),
                pl.BlockSpec((blocks, tile, block), lambda c, lens: (0, c, 0)),
                pl.BlockSpec((blocks, tile, block), lambda c, lens: (0, c, 0)),
                pl.BlockSpec((1, tile), lambda c, lens: (0, first + c)),
            ]
            + [pl.BlockSpec(memory_space=pl.ANY)] * len(old),
            out_specs=[
                pl.BlockSpec((1, tokens, tile), lambda c, lens: (first + c, 0, 0)),
                pl.BlockSpec((2, 2 * count, tile), lambda c, lens: (0, 0, c)),
            ],
        ),
        out_shape=[
            pltpu.VMEM((bias.shape[1] // tile, tokens, tile), F32),
            jax.ShapeDtypeStruct((2, 2 * count, tiles * tile), F32),
        ],
        input_output_aliases={5: 0} if old else {},
        compiler_params=pltpu.CompilerParams(vmem_limit_bytes=24 * 2**20),
        cost_estimate=NO_COST,
        name=f"forward{start}",
    )(lens, in_vmem(rows), *in_hbm(near), across, bias, *map(in_vmem, old))


def margins(parts, id_place, teachers, slopes, gathered):
    tiles, tokens, tile = slopes.shape
    queries, neg_count = teachers.shape
    pair = queries // 8
    n = len(gathered)
    ends = [sum(reps.shape[2] for reps in gathered[: i + 1]) // tile for i in range(n)]
    firsts = [0] + ends[:-1]
    batch = 4

    def kernel(s0, s1, s2, s3, ids, teach, slope, *refs):
        gathered, (margin, grad, coeff, coeff_t) = refs[:n], refs[n:]
        step = pl.program_id(0)

        @pl.when(step == 0)
        def _():
            score = (s0[...] + s1[...]) + (s2[...] + s3[...])
            lanes = lax.broadcasted_iota(jnp.int32, score.shape, 1)
            eye = lax.broadcasted_iota(jnp.int32, score.shape, 0) == lanes
            positive = jnp.sum(jnp.where(eye, score, 0.0), axis=1, keepdims=True)
            total = jnp.zeros_like(score)
            grad_pos = jnp.zeros_like(positive)
            for k in range(neg_count):
                chosen = ids[:, k : k + 1] == lanes
                negative = jnp.sum(jnp.where(chosen, score, 0.0), axis=1, keepdims=True)
                error = positive - negative - teach[:, k : k + 1]
                margin[:, k : k + 1] = error
                total = total - jnp.where(chosen, error, 0.0)
                grad_pos = grad_pos + error
            total = total + jnp.where(eye, grad_pos, 0.0)
            coeff[...] = total
            coeff_t[...] = total.T

        def fill(t, reps, first):
            there = pl.ds(pl.multiple_of((step * batch + t - first) * tile, tile), tile)
            here = pl.ds(pl.multiple_of((step * batch + t) * tile, tile), tile)
            grad_q = jnp.dot(
                coeff[:pair], reps[1, :, there], precision=HIGHEST, preferred_element_type=F32
            )
            grad_p = jnp.dot(
                coeff_t[:pair], reps[0, :, there], precision=HIGHEST, preferred_element_type=F32
            )
            at = 0
            for b in range(2):
                for span, part in ((LQ, grad_q), (LP, grad_p)):
                    for i in range(pair // 2):
                        row = b * (pair // 2) + i
                        grad[at : at + span, here] = (
                            slope[t, at : at + span, :] * part[row : row + 1]
                        ).astype(BF16)
                        at += span

        for t in range(batch):
            for reps, first, end in zip(gathered, firsts, ends):

                @pl.when((step * batch + t >= first) & (step * batch + t < end))
                def _():
                    fill(t, reps, first)

    square = pl.BlockSpec((queries, queries), lambda c: (0, 0))
    listed = pl.BlockSpec((queries, neg_count), lambda c: (0, 0))
    return pl.pallas_call(
        kernel,
        grid=(tiles // batch,),
        in_specs=[square] * 4
        + [listed] * 2
        + [pl.BlockSpec((batch, tokens, tile), lambda c: (c, 0, 0))]
        + [pl.BlockSpec(memory_space=pltpu.VMEM)] * n,
        out_specs=[listed, pl.BlockSpec(memory_space=pltpu.VMEM)],
        out_shape=[
            jax.ShapeDtypeStruct((queries, neg_count), F32),
            pltpu.VMEM((tokens, tiles * tile), BF16),
        ],
        scratch_shapes=[pltpu.VMEM((queries, queries), F32)] * 2,
        compiler_params=pltpu.CompilerParams(vmem_limit_bytes=24 * 2**20),
        name="margins",
    )(*parts, id_place, teachers, in_vmem(slopes), *gathered)


def back_piece(place, grads, heads, begin, steps):
    n = len(heads)
    rows, block = grads.shape[0], heads[0].shape[2]
    half = rows // 4

    def kernel(place, grad, *refs):
        heads, (send_x, keep_x, send_z, keep_z, total) = refs[:n], refs[n:]
        sums, start = None, 0
        for head in heads:
            wide = head.shape[1]
            part = jnp.dot(grad[:, start : start + wide], head[0], preferred_element_type=F32)
            sums = part if sums is None else sums + part
            start += wide
        total[...] = sums
        zlo, x = place[0], place[1]

        def rows_of(z, x):
            return total[pl.ds((2 * z + x) * half, half), :]

        @pl.when(pl.program_id(0) < steps // 2)
        def _():
            keep_x[0], keep_x[1] = rows_of(zlo, x), rows_of(1 - zlo, x)
            send_x[0] = rows_of(zlo, 1 - x).astype(BF16)
            send_x[1] = rows_of(1 - zlo, 1 - x).astype(BF16)

        @pl.when(pl.program_id(0) >= steps // 2)
        def _():
            keep_z[0], keep_z[1] = rows_of(zlo, x), rows_of(zlo, 1 - x)
            send_z[0] = rows_of(1 - zlo, x).astype(BF16)
            send_z[1] = rows_of(1 - zlo, 1 - x).astype(BF16)

    some = [
        pl.BlockSpec((1, h.shape[1], block), lambda d, place: (begin % 8 + d, 0, 0))
        for h in heads
    ]
    last = steps // 2 - 1
    by_x = pl.BlockSpec(
        (2, half, block), lambda d, place: (0, 0, jnp.minimum(d, last) ^ place[0])
    )
    by_z = pl.BlockSpec(
        (2, half, block), lambda d, place: (0, 0, jnp.maximum(d - last - 1, 0) ^ place[0])
    )
    shape = (2, half, steps // 2 * block)
    return pl.pallas_call(
        kernel,
        grid_spec=pltpu.PrefetchScalarGridSpec(
            num_scalar_prefetch=1,
            grid=(steps,),
            in_specs=[pl.BlockSpec(memory_space=pltpu.VMEM)] + some,
            out_specs=[by_x, by_x, by_z, by_z],
            scratch_shapes=[pltpu.VMEM((rows, block), F32)],
        ),
        out_shape=[pltpu.HBM(shape, t) for t in (BF16, F32, BF16, F32)],
        compiler_params=pltpu.CompilerParams(vmem_limit_bytes=24 * 2**20),
        cost_estimate=pl.CostEstimate(
            flops=2 * rows * grads.shape[1] * steps * block,
            bytes_accessed=2 * grads.shape[1] * steps * block + 3 * rows * steps * block,
            transcendentals=0,
        ),
        name=f"back{begin}",
    )(place, in_vmem(grads), *in_hbm(*heads))


def finish(places, pairs):
    rows = pairs[0][0].shape[0]
    widths = [pair[0].shape[1] for pair in pairs]
    block = sum(widths) // 16
    step = rows // 2

    def kernel(places, *refs):
        out = refs[-1]
        at = 0
        for i, width in enumerate(widths):
            for k in range(width // block):
                cols = slice(k * block, (k + 1) * block)
                lanes = pl.ds(pl.multiple_of(places[at + k] * block, block), block)
                out[:, lanes] = refs[2 * i][:, cols] + refs[2 * i + 1][:, cols].astype(F32)
            at += width // block

    return pl.pallas_call(
        kernel,
        grid_spec=pltpu.PrefetchScalarGridSpec(
            num_scalar_prefetch=1,
            grid=(rows // step,),
            in_specs=[
                pl.BlockSpec((step, width), lambda r, places: (r, 0)) for width in widths for _ in range(2)
            ],
            out_specs=pl.BlockSpec((step, 16 * block), lambda r, places: (r, 0)),
        ),
        out_shape=jax.ShapeDtypeStruct((rows, 16 * block), F32),
        compiler_params=pltpu.CompilerParams(vmem_limit_bytes=24 * 2**20),
        name="finish",
    )(places, *[a for pair in pairs for a in pair])


def by_squares(
    hidden, head_weight, head_bias, query_len, passage_len, neg_owner, neg_index, teacher
):
    count, neg_count = neg_owner.shape
    tokens, width = hidden.shape
    depth, columns = head_weight.shape
    share = columns // 2
    padded = -(-share // 256) * 256
    n = len(CHUNKS)
    starts = [sum(CHUNKS[:j]) for j in range(n)]
    me = lax.axis_index("dp")
    x = lax.axis_index("vocab")
    zlo = (me >> 2) & 1
    place = jnp.stack([zlo, x]).astype(jnp.int32)
    blocks = me ^ jnp.array(ORDER, jnp.int32)
    head = head_weight.T
    bias = jnp.pad(
        lax.dynamic_slice(head_bias, (zlo * share,), (share,)),
        (0, padded - share),
        constant_values=-1.0,
    )[None, :]
    half, piece = tokens // 2, tokens // 2 // len(HIDDEN)

    live = {}

    def columns_of(chunks, low):
        first, size = starts[chunks[0]], sum(CHUNKS[c] for c in chunks)
        return jnp.where(
            low == 0, head[first : first + size], head[share + first : share + first + size]
        )

    for k, chunks in NEAR.items():
        live["given", k] = columns_of(chunks, 1 - zlo)
    for i, k in enumerate(HIDDEN):
        live["hidden", k] = lax.dynamic_slice(hidden, (x * half + i * piece, 0), (piece, width))
    live["table"] = jnp.concatenate(
        [
            (neg_owner * count + neg_index).astype(F32),
            teacher,
            query_len[:, None].astype(F32),
            passage_len[:, None].astype(F32),
        ],
        axis=1,
    )

    def near_of(j):
        for k, chunks in NEAR.items():
            if j in chunks:
                first = starts[j] - starts[chunks[0]]
                return live["near", k][first : first + CHUNKS[j]]

    def beside(j):
        return jnp.concatenate([columns_of((j,), zlo), near_of(j)], axis=1)

    def reps_of(groups):
        return jnp.concatenate([live["reps", g] for g in groups], axis=2)

    rows = lens = slopes = None
    rounds = max(COMPUTED) + 2
    for k in range(rounds + 1):
        sent = {}
        if 0 <= k - 1 < n:
            j = k - 1
            if ("two", j) not in live:
                live["two", j] = beside(j)
            sent["far", j] = swap(live["two", j], ZHI)
            sent["side", j] = swap(live["two", j], Y)
        if 0 <= k - 2 < n:
            sent["beyond", k - 2] = swap(live["far", k - 2], Y)
        for i in NEAR:
            if k == max(i - (i == 1), 0):
                sent["near", i] = swap(live["given", i], ZLO)
        if k in HIDDEN:
            sent["from_z", k] = swap(live["hidden", k], ZLO)
        if k - 1 in HIDDEN:
            sent["from_x", k - 1] = swap(live["from_z", k - 1], X)
        if k - 1 in TABLE:
            table, came = live["table"], live["table came"]
            both = [table, came]
            if TABLE[k - 1] == ZLO:
                both = [jnp.where(zlo == 0, table, came), jnp.where(zlo == 0, came, table)]
            live["table"] = jnp.concatenate(both)
        if k in TABLE:
            sent["table came"] = swap(live["table"], TABLE[k])
        if k == max(HIDDEN) + 2:
            by_z, by_x = ([live[name, i] for i in HIDDEN] for name in ("from_z", "from_x"))
            rows = arrange(blocks, x, hidden, by_z, by_x)
            pair_lens = live["table"][: 2 * count, 2 * neg_count :].astype(jnp.int32)
            lens = pair_lens.reshape(2, count, 2).transpose(0, 2, 1).reshape(-1)
        for g in range(len(GROUPS)):
            if k == PACKED[g]:
                arrays = [live[name, j] for j in GROUPS[g] for name in ("two", "far", "side", "beyond")]
                sent["quads", g] = pack([arrays[4 * i : 4 * i + 4] for i in range(len(GROUPS[g]))])
            if k == MOVED[g]:
                quads = sent if k == PACKED[g] else live
                sent["across", g] = swap(quads["quads", g], CORE)
            if k == COMPUTED[g]:
                first = starts[GROUPS[g][0]]
                quads, across = (
                    sent[key] if key in sent else live[key] for key in (("quads", g), ("across", g))
                )
                slopes, sent["reps", g] = forward(lens, rows, quads, across, bias, slopes, first)
        for groups, first in GATHERED:
            if first is None or not 0 <= k - first <= 3:
                continue
            if k == first:
                own = reps_of(groups)
            else:
                own = jnp.concatenate([live["gathered", groups], live["came", groups]], axis=1)
            live["gathered", groups] = own
            if k - first < 3:
                sent["came", groups] = swap(own, (ZHI, Y, CORE)[k - first])
        live.update(sent)
        if k > max(COMPUTED):
            continue
        held = list(sent)
        if k == 0:
            held.remove(("near", 1))
        if k == 1:
            held.append(("near", 1))
        if any(k in chunks[1:] for chunks in NEAR.values()):
            live["two", k] = beside(k)
            held.append(("two", k))
        held += [key for key in (("given", k + 1), ("hidden", k + 1)) if key in live]
        live.update(zip(held, lax.optimization_barrier([live[key] for key in held])))
    ids = live["table"][:, :neg_count].astype(jnp.int32)
    teachers = live["table"][:, neg_count : 2 * neg_count]
    owner = ids // count
    order = jnp.array(ORDER[::2], jnp.int32)
    group = jnp.sum(
        jnp.where(((owner ^ me) & ~4)[:, :, None] == order, jnp.arange(8, dtype=jnp.int32), 0),
        axis=2,
    )
    id_place = (group * 2 + ((owner >> 2) & 1)) * count + ids % count

    late = reps_of(GATHERED[-1][0])
    late = jnp.concatenate([late] + [swap(late, bits) for bits in (ZHI, Y, ZHI | Y)], axis=1)
    late = jnp.concatenate([late, swap(late, CORE)], axis=1)
    gathered = [live["gathered", groups] for groups, _ in GATHERED[:-1]] + [late]

    def scores(reps):
        return lax.dot_general(reps[0], reps[1], (((1,), (1,)), ((), ())), precision=HIGHEST)

    part = sum(scores(reps) for reps in gathered)
    margin_error, grads = margins(
        (part, swap(part, X), swap(part, ZLO), swap(part, ZLO | X)),
        id_place,
        teachers,
        slopes,
        gathered,
    )

    pairs, first = [], [None] * len(PIECES)

    def second(i):
        (keep_x, came_x), (keep_z, came_z) = first[i]
        mids = [
            (keep[1] + came[1].astype(F32)).astype(BF16)
            for keep, came in ((keep_x, came_x), (keep_z, came_z))
        ]
        nonlocal grads
        mid_x, mid_z, grads = lax.optimization_barrier((*mids, grads))
        pairs.append((keep_x[0] + came_x[0].astype(F32), swap(mid_x, ZLO)))
        pairs.append((keep_z[0] + came_z[0].astype(F32), swap(mid_z, X)))

    for i, (begin, steps) in enumerate(PIECES):
        heads = [live["quads" if begin < 8 else "across", g] for g in range(len(GROUPS))]
        outs = back_piece(place, grads, heads, begin, steps)
        send_x, keep_x, send_z, keep_z, grads = lax.optimization_barrier((*outs, grads))
        first[i] = ((keep_x, swap(send_x, X)), (keep_z, swap(send_z, ZLO)))
        if i >= 1:
            second(i - 1)
    second(len(PIECES) - 1)
    places = []
    for k in range(0, 16, 2):
        base = (me & ~4) ^ ORDER[k]
        places += [base, base | 4]
    hidden_grad = finish(jnp.stack(places).astype(jnp.int32), pairs)
    return (lax.dynamic_slice(margin_error, (zlo * count, 0), (count, neg_count)), hidden_grad)


def solution(mesh):
    square = mesh.shape["dp"] == 16 and mesh.shape["vocab"] == 2
    return jax.shard_map(
        by_squares if square else any_mesh,
        mesh=mesh,
        in_specs=(
            P("dp", None),
            P("dp", "vocab"),
            P("vocab"),
            P("dp"),
            P("dp"),
            P("dp", None),
            P("dp", None),
            P("dp", None),
        ),
        out_specs=(P("dp", None), P(("dp", "vocab"), None)),
        check_vma=False,
    )
```
